256 devices in a mesh: dp: 4 (over x), expert: 8 (over z), tensor: 8 (over y, core).
Axes of the slice: x: 4, y: 4, z: 8, core: 2. Of those that a mesh axis runs over, the one named last changes fastest.
Arguments:
- tokens: bfloat16 [4096, 6144], P(('dp', 'expert')), may hold values from -6 to 6
- routes: int32 [4096, 2], P(('dp', 'expert')), may hold values from 0 to 7, as said below
- logits: float32 [4096, 2], P(('dp', 'expert')), may hold values from -6.5 to 6.5
- w_gate: bfloat16 [8, 6144, 8192], P('expert', None, ('dp', 'tensor')), may hold values from -0.078125 to 0.078125
- w_up: bfloat16 [8, 6144, 8192], P('expert', None, ('dp', 'tensor')), may hold values from -0.078125 to 0.078125
- w_down: bfloat16 [8, 8192, 6144], P('expert', ('dp', 'tensor')), may hold values from -0.0625 to 0.0625
Outputs:
- mixed: bfloat16 [4096, 6144], P(('dp', 'expert'), 'tensor')
The draws below stay inside these ranges and needn't reach their ends.
Inputs may be any that keep to these rules, and one draw needn't show every extreme that they name: `routes`: each row names two different experts. In each aligned block of 128 rows (the rows of one data shard) every expert is named, none more than 40 times, and five or six experts exactly 40 times.
All inputs are finite; a program needn't handle non-finite values.
Results may differ from the reference program's by a relative error of at most 0.025.
Values may be sent and summed in bfloat16 or wider, within the bound.
No kernel may reach another device: no remote copies, remote signals or barrier semaphores. Data moves between devices by JAX's collectives and lax.ppermute only.
A program may use at most 128 MiB of HBM per device.

```python
import jax
import jax.numpy as jnp
from jax import lax

D = 6144
FF = 8192
E = 8
TOK_DEV = 128
CAP = 40
TOKENS = 4096
N_DP = 4
N_TENSOR = 8


def draw_tokens(key, part):
    key = jax.random.fold_in(key, 1)
    values = jnp.clip(jax.random.normal(key, (TOKENS, D), jnp.float32), -6.0, 6.0)
    return values.astype(jnp.bfloat16)


def draw_logits(key, part):
    key = jax.random.fold_in(key, 2)
    centre_key, offset_key = jax.random.split(key, 2)
    centre = jnp.clip(2.0 * jax.random.normal(centre_key, (TOKENS,), jnp.float32), -6.0, 6.0)
    offset = jax.random.uniform(offset_key, (TOKENS,), jnp.float32, -0.3, 0.3)
    return jnp.stack([centre + 0.5 * offset, centre - 0.5 * offset], axis=1).astype(jnp.float32)


def draw_routes(key, part):
    key = jax.random.fold_in(key, 3)
    block_count = TOKENS // TOK_DEV
    block_keys = jax.random.split(key, block_count)

    def one_block(block_key):
        sub_keys = jax.random.split(block_key, 4)
        full_count = 5 + jax.random.randint(sub_keys[0], (), 0, 2)
        expert_order = jax.random.permutation(sub_keys[1], E).astype(jnp.int32)
        places = jnp.arange(E, dtype=jnp.int32)
        remaining = 2 * TOK_DEV - full_count * CAP
        other_count = E - full_count
        base_load = remaining // other_count
        extra_count = remaining % other_count
        load_counts = jnp.where(places < full_count, CAP, base_load + (places - full_count < extra_count).astype(jnp.int32))
        load_ends = jnp.cumsum(load_counts)
        positions = jnp.arange(2 * TOK_DEV, dtype=jnp.int32)
        slot_owner = jnp.sum((positions[:, None] >= load_ends[None, :]).astype(jnp.int32), axis=1)
        labels = expert_order[slot_owner]
        chosen_pairs = jnp.stack([labels[:TOK_DEV], labels[TOK_DEV:]], axis=1)
        shuffle = jax.random.permutation(sub_keys[2], TOK_DEV)
        chosen_pairs = chosen_pairs[shuffle]
        swap_bits = jax.random.randint(sub_keys[3], (TOK_DEV, 1), 0, 2)
        return jnp.where(swap_bits == 1, chosen_pairs[:, ::-1], chosen_pairs)
    return jax.vmap(one_block)(block_keys).reshape(TOKENS, 2).astype(jnp.int32)


def block_scale(rng, shape, cuts, smallest, high):
    def one(position, shards_of):
        heights = jax.random.uniform(jax.random.fold_in(jax.random.fold_in(rng, 6), position), (shards_of,), jnp.float32, smallest / len(cuts), high / len(cuts))
        return jnp.repeat(jnp.exp(heights), shape[position] // shards_of).reshape((-1,) + (1,) * (len(shape) - position - 1))

    level = one(*cuts[0])
    for cut in cuts[1:]:
        level = level * one(*cut)
    return level


def normal_values(key, shape, spread, bound, shards=(), kind=jnp.bfloat16):
    entries = jax.random.normal(key, shape, jnp.float32) * spread
    if len(shards) > 0:
        entries = block_scale(key, shape, shards, -0.22, 0.18) * entries
    return jnp.clip(entries, min=-bound, max=bound).astype(kind)


def setup_inputs(seed: int = 0) -> dict:
    seeds = jax.random.split(jax.random.key(seed), 7)
    tokens = draw_tokens(jax.random.fold_in(seeds[6], 71), 0)
    routes = draw_routes(jax.random.fold_in(seeds[6], 71), 0)
    logits = draw_logits(jax.random.fold_in(seeds[6], 71), 0)
    w_gate = normal_values(seeds[3], (E, D, FF), D ** -0.5, 0.078125, ((0, 8), (2, 32)))
    w_up = normal_values(seeds[4], (E, D, FF), D ** -0.5, 0.078125, ((0, 8), (2, 32)))
    w_down = normal_values(seeds[5], (E, FF, D), FF ** -0.5, 0.0625, ((0, 8), (1, 32)))
    return {"tokens": tokens, "routes": routes, "logits": logits, "w_gate": w_gate, "w_up": w_up, "w_down": w_down}


def reference(tokens, routes, logits, w_gate, w_up, w_down):
    total_rows = tokens.shape[0]
    blocks = total_rows // TOK_DEV
    choices = routes.reshape(blocks, TOK_DEV * 2)
    onehot = (choices[:, :, None] == jnp.arange(E, dtype=jnp.int32)[None, None, :]).astype(jnp.int32)
    before = jnp.cumsum(onehot, axis=1) - onehot
    slot_index = jnp.sum(before * onehot, axis=2).astype(jnp.int32)
    block_ids = jnp.broadcast_to(jnp.arange(blocks, dtype=jnp.int32)[:, None], (blocks, TOK_DEV * 2))
    expert_ids = choices.reshape(-1)
    block_flat = block_ids.reshape(-1)
    slot_flat = slot_index.reshape(-1)
    doubled = jnp.repeat(tokens, 2, axis=0)
    buffer = jnp.zeros((E, blocks, CAP, D), jnp.bfloat16)
    buffer = buffer.at[expert_ids, block_flat, slot_flat].set(doubled)
    groups = N_DP * N_TENSOR
    group_width = FF // groups
    row_count = blocks * CAP

    def expert(operands):
        slot_rows, gate_w, up_w, down_w = operands
        gate = jnp.dot(slot_rows, gate_w, preferred_element_type=jnp.float32)
        upper = jnp.dot(slot_rows, up_w, preferred_element_type=jnp.float32)
        hidden = (jax.nn.silu(gate) * upper).astype(jnp.bfloat16)
        hidden_groups = hidden.reshape(row_count, groups, group_width).transpose(1, 0, 2)
        down_groups = down_w.reshape(groups, group_width, D)

        def accumulate(running, pair):
            hidden_part, down_part = pair
            partial_value = jnp.dot(hidden_part, down_part, preferred_element_type=jnp.float32).astype(jnp.bfloat16)
            partial_value = lax.optimization_barrier(partial_value)
            return running + partial_value.astype(jnp.float32), None

        summed, _ = lax.scan(accumulate, jnp.zeros((row_count, D), jnp.float32), (hidden_groups, down_groups))
        return summed.astype(jnp.bfloat16)

    expert_out = lax.map(expert, (buffer.reshape(E, row_count, D), w_gate, w_up, w_down))
    expert_out = expert_out.reshape(E, blocks, CAP, D)
    picked = expert_out[expert_ids, block_flat, slot_flat]
    picked = lax.optimization_barrier(picked).astype(jnp.float32).reshape(total_rows, 2, D)
    share = jax.nn.sigmoid(logits - logits[:, ::-1])
    return jnp.sum(picked * share[:, :, None], axis=1).astype(jnp.bfloat16)
```

```python
import jax
import jax.numpy as jnp
from jax import lax
from jax.sharding import Mesh, PartitionSpec as P

E = 8
CAP = 40
BF = jnp.bfloat16
F32 = jnp.float32


def shift(value, axis, step):
    size = lax.axis_size(axis)
    return lax.ppermute(value, axis, [(i, (i + step) % size) for i in range(size)])


def spread(value, axis):
    return [value, shift(value, axis, 1), shift(value, axis, -1), shift(value, axis, 2)]


def gather_relay(value, axis, cut):
    below, above = shift(value, axis, 1), shift(value, axis, -1)
    first = shift(below[:cut], axis, 1)
    second = shift(above[cut:], axis, -1)
    return [value, below, above, jnp.concatenate([first, second], axis=0)]


def add_back(chunks, axis):
    parts = [chunks[0], shift(chunks[1], axis, -1), shift(chunks[2], axis, 1), shift(chunks[3], axis, 2)]
    return sum(p.astype(F32) for p in parts).astype(BF)


def body(tokens, routes, logits, w_gate, w_up, w_down):
    rows = tokens.shape[0]
    width = tokens.shape[1]
    half = width // 2
    part = half // 4
    y, c = lax.axis_index("ty"), lax.axis_index("core")
    swap = [(0, 1), (1, 0)]

    w_gate, w_up, w_down = w_gate[0], w_up[0], w_down[0]
    units = w_gate.shape[1]
    mine = lambda w: lax.dynamic_slice_in_dim(w, c * half, half, 0)
    other = lambda w: lax.dynamic_slice_in_dim(w, (1 - c) * half, half, 0)
    gate_theirs = lax.ppermute(other(w_gate), "core", swap)
    up_theirs = lax.ppermute(other(w_up), "core", swap)
    w_all = jnp.concatenate([mine(w_gate), gate_theirs, mine(w_up), up_theirs], axis=1)
    down = w_down.reshape(units, 4, 2, part)
    pick = lambda i: lax.dynamic_slice_in_dim(down, i, 1, 2)[:, :, 0]
    down_theirs = lax.ppermute(pick(1 - c), "core", swap)
    down_all = jnp.concatenate([pick(c), down_theirs], axis=0)

    offsets = [0, -1, 1, 2]
    order = [(y + o) % 4 for o in offsets]
    w_rel = [lax.dynamic_slice_in_dim(w_all, o * part, part, 0) for o in order]
    down_rel = [lax.dynamic_slice_in_dim(down_all, o, 1, 1)[:, 0] for o in order]

    expert_ids = routes.reshape(-1)
    onehot = (expert_ids[:, None] == jnp.arange(E, dtype=jnp.int32)[None, :]).astype(jnp.int32)
    before = jnp.cumsum(onehot, axis=0) - onehot
    slot_index = jnp.sum(before * onehot, axis=1)
    target = (expert_ids * CAP + slot_index).reshape(rows, 2)
    places = jnp.arange(E * CAP, dtype=jnp.int32)
    hit = places[:, None, None] == target[None, :, :]
    placing = jnp.any(hit, axis=2).astype(BF)
    columns = lax.dynamic_slice_in_dim(tokens, c * half + y * part, part, 1)
    outgoing = jnp.dot(placing, columns, preferred_element_type=F32).astype(BF)
    arrived = lax.all_to_all(outgoing.reshape(E, CAP, part), "expert", 0, 0, tiled=True)
    arrived = arrived.reshape(2, 4 * CAP, part)

    a_own = jnp.concatenate(spread(arrived[0], "dp"), axis=0)
    b_own = jnp.concatenate(spread(arrived[1], "ty"), axis=1)
    a_parts = gather_relay(a_own, "ty", 8 * CAP)
    b_parts = gather_relay(b_own, "dp", 2 * CAP)

    dot = lambda p, q: jnp.dot(p, q, preferred_element_type=F32)
    a_sum = sum(dot(p, w) for p, w in zip(a_parts, w_rel))
    w_flat = jnp.concatenate(w_rel, axis=0)
    b_sum = jnp.concatenate([dot(p, w_flat) for p in b_parts], axis=0)

    def hidden_of(total):
        blocks = [total[:, i * units : (i + 1) * units] for i in (1, 0, 3, 2)]
        sent = jnp.concatenate(blocks, axis=1).astype(BF)
        total = total + lax.ppermute(sent, "core", swap).astype(F32)
        gate, upper = total[:, : 2 * units], total[:, 2 * units :]
        return (jax.nn.silu(gate) * upper).astype(BF)

    a_hidden, b_hidden = hidden_of(a_sum), hidden_of(b_sum)

    a_out = [
        jnp.concatenate([dot(a_hidden[r * 160 : r * 160 + 160], d) for d in down_rel], axis=1).astype(BF)
        for r in range(4)
    ]
    b_out = [dot(b_hidden, d).astype(BF) for d in down_rel]
    a_mid = add_back(a_out, "dp")
    b_mid = add_back(b_out, "ty")
    a_end = add_back([a_mid[:, i * part : (i + 1) * part] for i in range(4)], "ty")
    b_end = add_back([b_mid[i * 160 : (i + 1) * 160] for i in range(4)], "dp")
    ready = jnp.concatenate([a_end, b_end], axis=0).reshape(E, CAP, part)
    table = lax.all_to_all(ready, "expert", 0, 0, tiled=True).reshape(E * CAP, part)

    share = jax.nn.sigmoid(logits - logits[:, ::-1])
    mix = jnp.sum(jnp.where(hit, share[None], 0.0), axis=2)
    high = mix.astype(BF)
    low = (mix - high.astype(F32)).astype(BF)
    back = lambda m: lax.dot_general(m, table, (((0,), (0,)), ((), ())), preferred_element_type=F32)
    return (back(high) + back(low)).astype(BF)


def solution(mesh):
    grid = Mesh(mesh.devices.reshape(4, 8, 4, 2), ("dp", "expert", "ty", "core"))
    tensor = ("ty", "core")
    placed = (
        P(("dp", "expert"), None),
        P(("dp", "expert"), None),
        P(("dp", "expert"), None),
        P("expert", None, ("dp",) + tensor),
        P("expert", None, ("dp",) + tensor),
        P("expert", ("dp",) + tensor, None),
    )
    return jax.shard_map(
        body, mesh=grid, in_specs=placed, out_specs=P(("dp", "expert"), tensor), check_vma=False
    )
```

```python
import jax
import jax.numpy as jnp
import numpy as np
from jax import lax
from jax.experimental import pallas as pl
from jax.experimental.pallas import tpu as pltpu
from jax.sharding import Mesh, PartitionSpec as P

E = 8
CAP = 40
BF = jnp.bfloat16
F32 = jnp.float32
OFFSETS = (0, -1, 1, 2)
ROUTES = ((0, 4), (1, -1), (2, -2), (3, -3))
MIB = 2**20


def dot(p, q):
    return jnp.dot(p, q, preferred_element_type=F32)


def plane(value, phase, step):
    pairs = []
    for x in range(4):
        for y in range(4):
            for c in range(2):
                along_x = (c == 0) == (phase == 0)
                to = ((x + step) % 4, y) if along_x else (x, (y + step) % 4)
                pairs.append(((x * 4 + y) * 2 + c, (to[0] * 4 + to[1]) * 2 + c))
    return lax.ppermute(value, ("dp", "ty", "core"), pairs)


def along_z(value, j):
    pairs = [(z * 4 + y, (z + ROUTES[y][j]) % 8 * 4 + y) for z in range(8) for y in range(4)]
    return lax.ppermute(value, ("expert", "ty"), pairs)


def swap(value):
    return lax.ppermute(value, "core", [(0, 1), (1, 0)])


def hidden_kernel(place, *refs):
    *parts, out = refs
    own, theirs = parts[:4], parts[4:]
    units = out.shape[1]
    block = own[0].shape[0] // 4
    for i in range(4):
        for j in range(4):
            total = own[i][j * block : (j + 1) * block, :]
            total = total + theirs[j][i * block : (i + 1) * block, :].astype(F32)
            gate, upper = total[:, :units], total[:, units:]
            value = gate / (1.0 + jnp.exp(-gate)) * upper
            start = pl.multiple_of(place[4 * i + j] * block, 16)
            out[pl.ds(start, block), :] = value.astype(BF)


def hidden_of(own, theirs, place):
    units = own[0].shape[1] // 2
    vmem = pl.BlockSpec(memory_space=pltpu.VMEM)
    return pl.pallas_call(
        hidden_kernel,
        in_specs=[pl.BlockSpec(memory_space=pltpu.SMEM)] + [vmem] * 8,
        out_specs=vmem,
        out_shape=jax.ShapeDtypeStruct((own[0].shape[0] * 4, units), BF),
        compiler_params=pltpu.CompilerParams(vmem_limit_bytes=40 * MIB),
    )(place, *own, *theirs)


def down_kernel(rows_of, cols_of, hidden, down, out):
    out[0, 0] = dot(hidden[...], down[0]).astype(BF)


def down_of(hidden, down, rows_of, cols_of, first, count):
    rows, units = hidden.shape
    rows, width = rows // 4, down.shape[2]
    return pl.pallas_call(
        down_kernel,
        grid_spec=pltpu.PrefetchScalarGridSpec(
            num_scalar_prefetch=2,
            grid=(count, 4),
            in_specs=[
                pl.BlockSpec((rows, units), lambda i, j, r, k: (r[(i + first) * 4 + j], 0)),
                pl.BlockSpec((1, units, width), lambda i, j, r, k: (k[(i + first) * 4 + j], 0, 0)),
            ],
            out_specs=pl.BlockSpec((1, 1, rows, width), lambda i, j, r, k: (i, j, 0, 0)),
        ),
        out_shape=jax.ShapeDtypeStruct((count, 4, rows, width), BF),
        compiler_params=pltpu.CompilerParams(vmem_limit_bytes=24 * MIB),
    )(rows_of, cols_of, hidden, down)


def last_kernel(order, a, b, c, d, out):
    out[...] = (a[...].astype(F32) + b[...].astype(F32) + c[...].astype(F32) + d[...].astype(F32)).astype(BF)


def last_sum(parts, order):
    shape = (E, CAP, parts[0].shape[-1])
    spec = pl.BlockSpec((1,) + shape[1:], lambda i, o: (o[i], 0, 0))
    return pl.pallas_call(
        last_kernel,
        grid_spec=pltpu.PrefetchScalarGridSpec(
            num_scalar_prefetch=1,
            grid=(E,),
            in_specs=[spec] * 4,
            out_specs=pl.BlockSpec((1,) + shape[1:], lambda i, o: (i, 0, 0)),
        ),
        out_shape=jax.ShapeDtypeStruct(shape, BF),
    )(order, *[p.reshape(shape) for p in parts])


def body(tokens, routes, logits, w_gate, w_up, w_down):
    rows, width = tokens.shape
    half = width // 2
    part = half // 4
    y, c, z = lax.axis_index("ty"), lax.axis_index("core"), lax.axis_index("expert")

    expert_ids = routes.reshape(-1)
    onehot = (expert_ids[:, None] == jnp.arange(E, dtype=jnp.int32)[None, :]).astype(jnp.int32)
    before = jnp.cumsum(onehot, axis=0) - onehot
    slot_index = jnp.sum(before * onehot, axis=1)
    target = (expert_ids * CAP + slot_index).reshape(rows, 2)
    columns = lax.dynamic_slice_in_dim(tokens, c * half, half, 1)
    steps = jnp.asarray(np.array(ROUTES, np.int32))[y]

    def outgoing(j):
        places = (z + steps[j] + 8) % 8 * CAP + jnp.arange(CAP, dtype=jnp.int32)
        hit = places[:, None, None] == target[None, :, :]
        return dot(jnp.any(hit, axis=2).astype(BF), columns).astype(BF)

    sent, w_gate, w_up, w_down = lax.optimization_barrier(
        ([outgoing(0), outgoing(1)], w_gate, w_up, w_down)
    )
    arrived = [along_z(sent[j], j) for j in range(2)]

    w_gate, w_up, w_down = w_gate[0], w_up[0], w_down[0]
    units = w_gate.shape[1]
    mine = lambda w: lax.dynamic_slice_in_dim(w, c * half, half, 0)
    other = lambda w: lax.dynamic_slice_in_dim(w, (1 - c) * half, half, 0)
    down = w_down.reshape(units, 4, 2, part)
    pick = lambda i: lax.dynamic_slice_in_dim(down, i, 1, 2)[:, :, 0].transpose(1, 0, 2)
    theirs = [swap(other(w_gate)), swap(other(w_up)), swap(pick(1 - c))]
    arrived, theirs = lax.optimization_barrier((arrived, theirs))
    w_all = jnp.concatenate([mine(w_gate), theirs[0], mine(w_up), theirs[1]], axis=1)
    down_all = jnp.concatenate([pick(c), theirs[2]], axis=1)

    piece = jnp.concatenate(arrived, axis=0)
    slab = jnp.concatenate(
        [piece, plane(piece, 0, 1), plane(piece, 0, -1), plane(piece, 0, 2)], axis=0
    )
    below, above = plane(slab, 1, 1), plane(slab, 1, -1)
    cut = slab.shape[0] // 2
    far = [plane(below[:cut], 1, 1), plane(above[cut:], 1, -1)]

    own = [dot(slab, w_all), dot(below, w_all), dot(above, w_all)]
    own.append(jnp.concatenate([dot(f, w_all) for f in far], axis=0))

    def exchange(total):
        blocks = [total[:, i * units : (i + 1) * units] for i in (1, 0, 3, 2)]
        return swap(jnp.concatenate(blocks, axis=1).astype(BF))

    offsets = jnp.asarray(np.array(OFFSETS, np.int32))
    lines = (y + offsets + 4) % 4
    i4 = jnp.arange(4, dtype=jnp.int32)
    place = jnp.where(c == 0, i4[None, :] * 4 + lines[:, None], i4[:, None] * 4 + lines[None, :])
    hidden = hidden_of(own, [exchange(t) for t in own], place.reshape(-1))

    first = jnp.broadcast_to(i4[:, None], (4, 4))
    second = jnp.broadcast_to(i4[None, :], (4, 4))
    rows_of = jnp.where(c == 0, first, second).reshape(-1)
    cols_of = jnp.where(c == 0, lines[second], lines[first]).reshape(-1)
    [far_out] = down_of(hidden, down_all, rows_of, cols_of, 3, 1)
    near_out = down_of(hidden, down_all, rows_of, cols_of, 0, 3)

    from_below, from_above = plane(far_out[:2], 0, 1), plane(far_out[2:], 0, -1)
    add = lambda *v: sum(a.astype(F32) for a in v).astype(BF)
    to_above = jnp.concatenate([add(near_out[2, :2], from_below), near_out[2, 2:]], axis=0)
    to_below = jnp.concatenate([near_out[1, :2], add(near_out[1, 2:], from_above)], axis=0)
    mid = add(near_out[0], plane(to_above, 0, 1), plane(to_below, 0, -1))
    ends = [mid[0], plane(mid[1], 1, -1), plane(mid[2], 1, 1), plane(mid[3], 1, 2)]
    inverse = np.zeros(8, np.int32)
    for i, s in enumerate(sum(ROUTES, ())):
        inverse[s % 8] = i
    order = jnp.asarray(inverse)[(z - jnp.arange(8, dtype=jnp.int32) + 8) % 8]
    ready = last_sum(ends, order)
    table = lax.all_to_all(ready, "expert", 0, 0, tiled=True).reshape(E * CAP, part)

    share = jax.nn.sigmoid(logits - logits[:, ::-1])
    places = jnp.arange(E * CAP, dtype=jnp.int32)
    hit = places[:, None, None] == target[None, :, :]
    mix = jnp.sum(jnp.where(hit, share[None], 0.0), axis=2)
    high = mix.astype(BF)
    low = (mix - high.astype(F32)).astype(BF)
    back = lambda m: lax.dot_general(m, table, (((0,), (0,)), ((), ())), preferred_element_type=F32)
    return (back(high) + back(low)).astype(BF)


def solution(mesh):
    grid = Mesh(mesh.devices.reshape(4, 8, 4, 2), ("dp", "expert", "ty", "core"))
    tensor = ("ty", "core")
    placed = (
        P(("dp", "expert"), None),
        P(("dp", "expert"), None),
        P(("dp", "expert"), None),
        P("expert", None, ("dp",) + tensor),
        P("expert", None, ("dp",) + tensor),
        P("expert", ("dp",) + tensor, None),
    )
    return jax.shard_map(
        body, mesh=grid, in_specs=placed, out_specs=P(("dp", "expert"), tensor), check_vma=False
    )
```

```python
import functools

import jax
import jax.numpy as jnp
import numpy as np
from jax import lax
from jax.experimental import pallas as pl
from jax.experimental.pallas import tpu as pltpu
from jax.sharding import Mesh, PartitionSpec as P

E = 8
CAP = 40
BF = jnp.bfloat16
F32 = jnp.float32
OFFSETS = (0, -1, 1, 2)
ROUTES = ((0, 4), (1, -1), (2, -2), (3, -3))
MIB = 2**20
VMEM = pl.BlockSpec(memory_space=pltpu.VMEM)
SMEM = pl.BlockSpec(memory_space=pltpu.SMEM)
ANY = pl.BlockSpec(memory_space=pl.ANY)
HBM = pl.BlockSpec(memory_space=pltpu.HBM)
COST = pl.CostEstimate(flops=MIB, bytes_accessed=MIB, transcendentals=0)


def dot(p, q):
    return jnp.dot(p, q, preferred_element_type=F32)


def add(*values):
    return sum(v.astype(F32) for v in values).astype(BF)


def plane(value, phase, step):
    pairs = []
    for x in range(4):
        for y in range(4):
            for c in range(2):
                along_x = (c == 0) == (phase == 0)
                to = ((x + step) % 4, y) if along_x else (x, (y + step) % 4)
                pairs.append(((x * 4 + y) * 2 + c, (to[0] * 4 + to[1]) * 2 + c))
    return lax.ppermute(value, ("dp", "ty", "core"), pairs)


def along_z(value, j):
    pairs = [(z * 4 + y, (z + ROUTES[y][j]) % 8 * 4 + y) for z in range(8) for y in range(4)]
    return lax.ppermute(value, ("expert", "ty"), pairs)


def swap(value):
    return lax.ppermute(value, "core", [(0, 1), (1, 0)])


def after(value, *others):
    return pl.pallas_call(
        lambda *refs: None,
        in_specs=[ANY] * (1 + len(others)),
        out_specs=ANY,
        out_shape=jax.ShapeDtypeStruct(value.shape, value.dtype),
        input_output_aliases={0: 0},
        compiler_params=pltpu.CompilerParams(vmem_limit_bytes=MIB),
        cost_estimate=COST,
    )(value, *others)


def gate_up_kernel(pieces, scalars, *refs):
    rows, weights = refs[:pieces], refs[pieces : pieces + 4]
    out, held, weight, row_sems, sems = refs[-5:]
    depth, step = weight.shape[1:]
    at, row_copies = 0, []
    for i, ref in enumerate(rows):
        count = ref.shape[0]
        row_copies.append(pltpu.make_async_copy(ref, held.at[pl.ds(at, count)], row_sems.at[i]))
        at += count
    start = pl.multiple_of(scalars[20] * depth, depth)
    copies = [
        pltpu.make_async_copy(ref.at[pl.ds(start, depth)], weight.at[i], sems.at[i])
        for i, ref in enumerate(weights)
    ]
    for copy in row_copies + copies:
        copy.start()
    for copy in row_copies:
        copy.wait()

    @pl.loop(0, 4)
    def _(n):
        pltpu.make_async_copy(weights[0].at[pl.ds(start, depth)], weight.at[n], sems.at[n]).wait()
        value = dot(held[...], weight[n])
        column = pl.multiple_of(n * step, step)
        for i in range(out.shape[0]):
            block = value[i * out.shape[1] : (i + 1) * out.shape[1]]
            out[i, :, pl.ds(column, step)] = block.astype(BF)


def gate_up(rows, weights, scalars):
    count = sum(r.shape[0] for r in rows)
    depth, step = weights[0].shape
    depth //= 2
    block = 2 * CAP
    return pl.pallas_call(
        functools.partial(gate_up_kernel, len(rows)),
        in_specs=[SMEM] + [ANY] * len(rows) + [HBM] * 4,
        out_specs=VMEM,
        out_shape=jax.ShapeDtypeStruct((count // block, block, 4 * step), BF),
        scratch_shapes=[
            pltpu.VMEM((count, depth), BF),
            pltpu.VMEM((4, depth, step), BF),
            pltpu.SemaphoreType.DMA((len(rows),)),
            pltpu.SemaphoreType.DMA((4,)),
        ],
        compiler_params=pltpu.CompilerParams(vmem_limit_bytes=24 * MIB),
        cost_estimate=COST,
    )(scalars, *rows, *weights)


def down_copies(scalars, mine, theirs, down, sems, count=4):
    units, part = mine.shape[0], down.shape[2]
    copies = []
    for k in range(count):
        start = pl.multiple_of((2 * scalars[16 + k] + scalars[20]) * part, part)
        for side, ref in enumerate((mine, theirs)):
            copies.append(
                pltpu.make_async_copy(
                    ref.at[:, pl.ds(start, part)],
                    down.at[k, pl.ds(side * units, units)],
                    sems.at[2 * k + side],
                )
            )
    return copies


def hidden_kernel(
    scalars, sums, got, mine, theirs, hidden, far_a, far_b, down, sems
):
    copies = down_copies(scalars, mine, theirs, down, sems)
    for copy in copies:
        copy.start()
    units = hidden.shape[1] // 2
    rows = hidden.shape[0] // 4
    block = rows // 4
    for i in range(4):
        for j in range(4):
            start = pl.multiple_of(scalars[4 * i + j] * block, 16)
            here, there = sums[4 * i + j].astype(F32), got[4 * j + i].astype(F32)
            for side in range(2):
                at, other = 2 * units * side, 2 * units * (1 - side)
                gate = here[:, at : at + units] + there[:, other : other + units]
                upper = here[:, at + units : at + 2 * units]
                upper = upper + there[:, other + units : other + 2 * units]
                value = gate / (1.0 + jnp.exp(-gate)) * upper
                hidden[pl.ds(start, block), side * units : (side + 1) * units] = value.astype(BF)
    outs = (far_a.at[0], far_a.at[1], far_b.at[0], far_b.at[1])
    for copy in copies:
        copy.wait()

    @pl.when(scalars[20] == 0)
    def _():
        for k in range(4):
            outs[k][...] = dot(hidden[3 * rows :, :], down[k]).astype(BF)

    @pl.when(scalars[20] == 1)
    def _():
        value = dot(hidden[...], down[3]).astype(BF)
        for r in range(4):
            outs[r][...] = value[r * rows : (r + 1) * rows]


def hidden_of(sums, got, mine, theirs, scalars):
    rows, units = sums.shape[0] * sums.shape[1], 2 * mine.shape[0]
    part = mine.shape[1] // 8
    piece = jax.ShapeDtypeStruct((2, rows // 4, part), BF)
    return pl.pallas_call(
        hidden_kernel,
        in_specs=[SMEM] + [VMEM] * 2 + [HBM] * 2,
        out_specs=[VMEM] * 3,
        out_shape=[jax.ShapeDtypeStruct((rows, units), BF), piece, piece],
        scratch_shapes=[pltpu.VMEM((4, units, part), BF), pltpu.SemaphoreType.DMA((8,))],
        compiler_params=pltpu.CompilerParams(vmem_limit_bytes=20 * MIB),
        cost_estimate=COST,
    )(scalars, sums, got, mine, theirs)


def down_kernel(
    scalars, hidden, mine, theirs, below_a, below_b, above_a, above_b, own, down, sems
):
    copies = down_copies(scalars, mine, theirs, down, sems)
    for copy in copies:
        copy.start()
    for copy in copies:
        copy.wait()
    rows = hidden.shape[0] // 4
    outs = (
        (own.at[0], own.at[1], own.at[2], own.at[3]),
        (below_a.at[0], below_a.at[1], below_b.at[0], below_b.at[1]),
        (above_a.at[0], above_a.at[1], above_b.at[0], above_b.at[1]),
    )

    @pl.when(scalars[20] == 0)
    def _():
        for k in range(4):
            value = dot(hidden[: 3 * rows, :], down[k]).astype(BF)
            for r in range(3):
                outs[r][k][...] = value[r * rows : (r + 1) * rows]

    @pl.when(scalars[20] == 1)
    def _():
        for k in range(3):
            value = dot(hidden[...], down[k]).astype(BF)
            for r in range(4):
                outs[k][r][...] = value[r * rows : (r + 1) * rows]


def down_of(hidden, mine, theirs, scalars):
    rows, units = hidden.shape
    part = mine.shape[1] // 8
    return pl.pallas_call(
        down_kernel,
        in_specs=[SMEM, VMEM, HBM, HBM],
        out_specs=[VMEM] * 5,
        out_shape=[jax.ShapeDtypeStruct((s, rows // 4, part), BF) for s in (2, 2, 2, 2, 4)],
        scratch_shapes=[pltpu.VMEM((4, units, part), BF), pltpu.SemaphoreType.DMA((8,))],
        compiler_params=pltpu.CompilerParams(vmem_limit_bytes=20 * MIB),
        cost_estimate=COST,
    )(scalars, hidden, mine, theirs)


def body(tokens, routes, logits, w_gate, w_up, w_down):
    rows, width = tokens.shape
    half = width // 2
    part = half // 4
    y, c, z = lax.axis_index("ty"), lax.axis_index("core"), lax.axis_index("expert")

    expert_ids = routes.reshape(-1)
    onehot = (expert_ids[:, None] == jnp.arange(E, dtype=jnp.int32)[None, :]).astype(jnp.int32)
    before = jnp.cumsum(onehot, axis=0) - onehot
    slot_index = jnp.sum(before * onehot, axis=1)
    target = (expert_ids * CAP + slot_index).reshape(rows, 2)
    columns = lax.dynamic_slice_in_dim(tokens, c * half, half, 1)
    slots = jnp.arange(CAP, dtype=jnp.int32)

    def outgoing(j):
        step = jnp.int32(ROUTES[0][j])
        for line in range(1, 4):
            step = jnp.where(y == line, ROUTES[line][j], step)
        places = (z + step + 8) % 8 * CAP + slots
        hit = places[:, None, None] == target[None, :, :]
        return dot(jnp.any(hit, axis=2).astype(BF), columns).astype(BF)

    w_gate, w_up, w_down = w_gate[0], w_up[0], w_down[0]
    weights = [w_gate, w_up, swap(w_gate), swap(w_up)]
    downs = [w_down, swap(w_down)]
    arrived = [along_z(outgoing(j), j) for j in range(2)]
    piece = after(jnp.concatenate(arrived, axis=0), *weights[2:], downs[1])

    lines = [(y + o + 4) % 4 for o in OFFSETS]
    place = [jnp.where(c == 0, j * 4 + lines[i], i * 4 + lines[j]) for i in range(4) for j in range(4)]
    scalars = jnp.stack(place + lines + [c] + [jnp.int32(0)] * 3).astype(jnp.int32)

    low = jnp.concatenate([piece, plane(piece, 0, 1)], axis=0)
    high = jnp.concatenate([plane(piece, 0, -1), plane(piece, 0, 2)], axis=0)
    below_low, above_high = plane(low, 1, 1), plane(high, 1, -1)
    below_high, above_low = plane(high, 1, 1), plane(low, 1, -1)
    far = [plane(below_low, 1, 1), plane(above_high, 1, -1)]
    rows_all = [low, high, below_low, below_high, above_low, above_high, *far]
    sums = gate_up(rows_all, weights, scalars)
    hidden, far_a, far_b = hidden_of(sums, swap(sums), *downs, scalars)
    below_a, below_b, above_a, above_b, own = down_of(hidden, *downs, scalars)

    from_below, from_above = plane(far_a, 0, 1), plane(far_b, 0, -1)
    got_high, got_low = plane(above_b, 0, 1), plane(below_a, 0, -1)
    got_low2 = plane(add(above_a, from_below), 0, 1)
    got_high2 = plane(add(below_b, from_above), 0, -1)
    mid = [add(own[i], got_low[i], got_low2[i]) for i in range(2)]
    mid += [add(own[2 + i], got_high[i], got_high2[i]) for i in range(2)]
    ends = [mid[0], plane(mid[1], 1, -1), plane(mid[2], 1, 1), plane(mid[3], 1, 2)]
    moved = []
    for step in range(0, -8, -1):
        [found] = [(i, j) for i in range(4) for j in range(2) if (ROUTES[i][j] - step) % 8 == 0]
        at = (2 * found[0] + found[1]) * CAP
        moved.append(add(*[e[at : at + CAP] for e in ends]))
    moved = jnp.concatenate(moved * 2, axis=0).reshape(2 * E, CAP, part)
    moved = lax.dynamic_slice_in_dim(moved, (E - z) % E, E, 0)
    table = lax.all_to_all(moved, "expert", 0, 0, tiled=True).reshape(E * CAP, part)

    share = jax.nn.sigmoid(logits - logits[:, ::-1])
    hit = jnp.arange(E * CAP, dtype=jnp.int32)[None, :, None] == target[:, None, :]
    mix = jnp.sum(jnp.where(hit, share[:, None, :], 0.0), axis=2)
    high_mix = mix.astype(BF)
    low_mix = (mix - high_mix.astype(F32)).astype(BF)
    return (dot(high_mix, table) + dot(low_mix, table)).astype(BF)


def solution(mesh):
    grid = Mesh(mesh.devices.reshape(4, 8, 4, 2), ("dp", "expert", "ty", "core"))
    tensor = ("ty", "core")
    placed = (
        P(("dp", "expert"), None),
        P(("dp", "expert"), None),
        P(("dp", "expert"), None),
        P("expert", None, ("dp",) + tensor),
        P("expert", None, ("dp",) + tensor),
        P("expert", ("dp",) + tensor, None),
    )
    return jax.shard_map(
        body, mesh=grid, in_specs=placed, out_specs=P(("dp", "expert"), tensor), check_vma=False
    )
```

```python
import functools

import jax
import jax.numpy as jnp
import numpy as np
from jax import lax
from jax.experimental import pallas as pl
from jax.experimental.pallas import tpu as pltpu
from jax.sharding import Mesh, PartitionSpec as P

E = 8
CAP = 40
BF = jnp.bfloat16
F32 = jnp.float32
OFFSETS = (0, -1, 1, 2)
ROUTES = ((0, 4), (1, -1), (2, -2), (3, -3))
MIB = 2**20
VMEM = pl.BlockSpec(memory_space=pltpu.VMEM)
SMEM = pl.BlockSpec(memory_space=pltpu.SMEM)
ANY = pl.BlockSpec(memory_space=pl.ANY)
HBM = pl.BlockSpec(memory_space=pltpu.HBM)
COST = pl.CostEstimate(flops=MIB, bytes_accessed=MIB, transcendentals=0)


def dot(p, q):
    return jnp.dot(p, q, preferred_element_type=F32)


def add(*values):
    return sum(v.astype(F32) for v in values).astype(BF)


def plane(value, phase, step):
    pairs = []
    for x in range(4):
        for y in range(4):
            for c in range(2):
                along_x = (c == 0) == (phase == 0)
                to = ((x + step) % 4, y) if along_x else (x, (y + step) % 4)
                pairs.append(((x * 4 + y) * 2 + c, (to[0] * 4 + to[1]) * 2 + c))
    return lax.ppermute(value, ("dp", "ty", "core"), pairs)


def along_z(value, j):
    pairs = []
    for z in range(8):
        for y in range(4):
            for c in range(2):
                to = (z + ROUTES[-y % 4 if c else y][j]) % 8
                pairs.append(((z * 4 + y) * 2 + c, (to * 4 + y) * 2 + c))
    return lax.ppermute(value, ("expert", "ty", "core"), pairs)


def swap(value):
    return lax.ppermute(value, "core", [(0, 1), (1, 0)])


def after(value, *others):
    return pl.pallas_call(
        lambda *refs: None,
        in_specs=[ANY] * (1 + len(others)),
        out_specs=ANY,
        out_shape=jax.ShapeDtypeStruct(value.shape, value.dtype),
        input_output_aliases={0: 0},
        compiler_params=pltpu.CompilerParams(vmem_limit_bytes=MIB),
        cost_estimate=COST,
    )(value, *others)


def gate_up_kernel(places, merges, scalars, *refs):
    pieces = len(places)
    rows, weights, before = refs[:pieces], refs[pieces : pieces + 4], refs[pieces + 4 : -6]
    out, held, weight, row_sems, sems, merge_sems = refs[-6:]
    depth, step = weight.shape[1:]
    block = out.shape[1]
    start = pl.multiple_of(scalars[20] * depth, depth)
    at, row_copies, order = 0, [], []
    for i, (ref, place) in enumerate(zip(rows, places)):
        count = ref.shape[0]
        row_copies.append(pltpu.make_async_copy(ref, held.at[pl.ds(at, count)], row_sems.at[i]))
        at += count
        order += range(place, place + count // block)
    copies = [
        pltpu.make_async_copy(ref.at[pl.ds(start, depth)], weight.at[i], sems.at[i])
        for i, ref in enumerate(weights)
    ]
    merge_copies = [
        pltpu.make_async_copy(
            before[n].at[pl.ds(first, 2)], out.at[pl.ds(to, 2)], merge_sems.at[i]
        )
        for i, (n, first, to) in enumerate(merges)
    ]
    for copy in row_copies + copies + merge_copies:
        copy.start()
    for copy in row_copies:
        copy.wait()

    @pl.loop(0, 4)
    def _(n):
        pltpu.make_async_copy(weights[0].at[pl.ds(start, depth)], weight.at[n], sems.at[n]).wait()
        value = dot(held[...], weight[n])
        column = pl.multiple_of(n * step, step)
        for i, place in enumerate(order):
            out[place, :, pl.ds(column, step)] = value[i * block : (i + 1) * block].astype(BF)

    for copy in merge_copies:
        copy.wait()


def gate_up(rows, places, weights, scalars, before=(), merges=()):
    count, block = sum(r.shape[0] for r in rows), 2 * CAP
    depth, step = weights[0].shape
    depth //= 2
    blocks = count // block + 2 * len(merges)
    return pl.pallas_call(
        functools.partial(gate_up_kernel, places, merges),
        in_specs=[SMEM] + [ANY] * len(rows) + [HBM] * 4 + [ANY] * len(before),
        out_specs=VMEM,
        out_shape=jax.ShapeDtypeStruct((blocks, block, 4 * step), BF),
        scratch_shapes=[
            pltpu.VMEM((count, depth), BF),
            pltpu.VMEM((4, depth, step), BF),
            pltpu.SemaphoreType.DMA((len(rows),)),
            pltpu.SemaphoreType.DMA((4,)),
            pltpu.SemaphoreType.DMA((max(len(merges), 1),)),
        ],
        compiler_params=pltpu.CompilerParams(vmem_limit_bytes=20 * MIB),
        cost_estimate=COST,
    )(scalars, *rows, *weights, *before)


def down_copies(scalars, mine, theirs, down, sems, count=4):
    units, part = mine.shape[0], down.shape[2]
    copies = []
    for k in range(count):
        start = pl.multiple_of((2 * scalars[16 + k] + scalars[20]) * part, part)
        for side, ref in enumerate((mine, theirs)):
            copies.append(
                pltpu.make_async_copy(
                    ref.at[:, pl.ds(start, part)],
                    down.at[k, pl.ds(side * units, units)],
                    sems.at[2 * k + side],
                )
            )
    return copies


def hidden_kernel(
    scalars, sums, got, mine, theirs, hidden, far_a, far_b, down, sems
):
    copies = down_copies(scalars, mine, theirs, down, sems)
    for copy in copies:
        copy.start()
    units = hidden.shape[1] // 2
    rows = hidden.shape[0] // 4
    block = rows // 4
    for i in range(16):
        here, there = sums[scalars[i]].astype(F32), got[scalars[24 + i]].astype(F32)
        for side in range(2):
            at, other = 2 * units * side, 2 * units * (1 - side)
            gate = here[:, at : at + units] + there[:, other : other + units]
            upper = here[:, at + units : at + 2 * units]
            upper = upper + there[:, other + units : other + 2 * units]
            value = gate / (1.0 + jnp.exp(-gate)) * upper
            hidden[i * block : (i + 1) * block, side * units : (side + 1) * units] = value.astype(BF)
    outs = (far_a.at[0], far_a.at[1], far_b.at[0], far_b.at[1])
    for copy in copies:
        copy.wait()

    @pl.when(scalars[20] == 0)
    def _():
        for k in range(4):
            outs[k][...] = dot(hidden[3 * rows :, :], down[k]).astype(BF)

    @pl.when(scalars[20] == 1)
    def _():
        value = dot(hidden[...], down[3]).astype(BF)
        for r in range(4):
            outs[r][...] = value[r * rows : (r + 1) * rows]


def hidden_of(sums, got, mine, theirs, scalars):
    rows, units = sums.shape[0] * sums.shape[1], 2 * mine.shape[0]
    part = mine.shape[1] // 8
    piece = jax.ShapeDtypeStruct((2, rows // 4, part), BF)
    return pl.pallas_call(
        hidden_kernel,
        in_specs=[SMEM] + [VMEM] * 2 + [HBM] * 2,
        out_specs=[VMEM] * 3,
        out_shape=[jax.ShapeDtypeStruct((rows, units), BF), piece, piece],
        scratch_shapes=[pltpu.VMEM((4, units, part), BF), pltpu.SemaphoreType.DMA((8,))],
        compiler_params=pltpu.CompilerParams(vmem_limit_bytes=20 * MIB),
        cost_estimate=COST,
    )(scalars, sums, got, mine, theirs)


def down_kernel(
    scalars, hidden, mine, theirs, below_a, below_b, above_a, above_b, own, down, sems
):
    copies = down_copies(scalars, mine, theirs, down, sems)
    for copy in copies:
        copy.start()
    for copy in copies:
        copy.wait()
    rows = hidden.shape[0] // 4
    outs = (
        (own.at[0], own.at[1], own.at[2], own.at[3]),
        (below_a.at[0], below_a.at[1], below_b.at[0], below_b.at[1]),
        (above_a.at[0], above_a.at[1], above_b.at[0], above_b.at[1]),
    )

    @pl.when(scalars[20] == 0)
    def _():
        for k in range(4):
            value = dot(hidden[: 3 * rows, :], down[k]).astype(BF)
            for r in range(3):
                outs[r][k][...] = value[r * rows : (r + 1) * rows]

    @pl.when(scalars[20] == 1)
    def _():
        for k in range(3):
            value = dot(hidden[...], down[k]).astype(BF)
            for r in range(4):
                outs[k][r][...] = value[r * rows : (r + 1) * rows]


def down_of(hidden, mine, theirs, scalars):
    rows, units = hidden.shape
    part = mine.shape[1] // 8
    return pl.pallas_call(
        down_kernel,
        in_specs=[SMEM, VMEM, HBM, HBM],
        out_specs=[VMEM] * 5,
        out_shape=[jax.ShapeDtypeStruct((s, rows // 4, part), BF) for s in (2, 2, 2, 2, 4)],
        scratch_shapes=[pltpu.VMEM((4, units, part), BF), pltpu.SemaphoreType.DMA((8,))],
        compiler_params=pltpu.CompilerParams(vmem_limit_bytes=20 * MIB),
        cost_estimate=COST,
    )(scalars, hidden, mine, theirs)


def mid_kernel(own, high, low, got_1, got_2, mid_1, mid_2):
    for i, parts, out in ((1, (low.at[1], got_1), mid_1), (2, (high.at[0], got_2), mid_2)):
        total = own[i].astype(F32)
        for part in parts:
            total = total + part[...].astype(F32)
        out[...] = total.astype(BF)


def mid_sums(*values):
    piece = jax.ShapeDtypeStruct(values[-1].shape, BF)
    return pl.pallas_call(
        mid_kernel,
        in_specs=[VMEM] * 5,
        out_specs=[VMEM] * 2,
        out_shape=[piece, piece],
        compiler_params=pltpu.CompilerParams(vmem_limit_bytes=16 * MIB),
        cost_estimate=COST,
    )(*values)


def last_kernel(places, a, b, c, d, out):
    for i in range(E):
        total = a[i].astype(F32) + b[i].astype(F32) + c[i].astype(F32) + d[i].astype(F32)
        out[places[i]] = total.astype(BF)


def last_sum(places, parts):
    shape = (E, CAP, parts[0].shape[1])
    return pl.pallas_call(
        last_kernel,
        in_specs=[SMEM] + [VMEM] * 4,
        out_specs=VMEM,
        out_shape=jax.ShapeDtypeStruct(shape, BF),
        compiler_params=pltpu.CompilerParams(vmem_limit_bytes=16 * MIB),
        cost_estimate=COST,
    )(places, *[p.reshape(shape) for p in parts])


def body(tokens, routes, logits, w_gate, w_up, w_down):
    rows, width = tokens.shape
    half = width // 2
    part = half // 4
    y, c, z = lax.axis_index("ty"), lax.axis_index("core"), lax.axis_index("expert")

    expert_ids = routes.reshape(-1)
    onehot = (expert_ids[:, None] == jnp.arange(E, dtype=jnp.int32)[None, :]).astype(jnp.int32)
    before = jnp.cumsum(onehot, axis=0) - onehot
    slot_index = jnp.sum(before * onehot, axis=1)
    target = (expert_ids * CAP + slot_index).reshape(rows, 2)
    columns = lax.dynamic_slice_in_dim(tokens, c * half, half, 1)
    slots = jnp.arange(CAP, dtype=jnp.int32)
    line = jnp.where(c == 0, y, -y % 4)

    def outgoing(j):
        step = jnp.int32(ROUTES[0][j])
        for number in range(1, 4):
            step = jnp.where(line == number, ROUTES[number][j], step)
        places = (z + step + 8) % 8 * CAP + slots
        hit = places[:, None, None] == target[None, :, :]
        return dot(jnp.any(hit, axis=2).astype(BF), columns).astype(BF)

    w_gate, w_up, w_down = w_gate[0], w_up[0], w_down[0]
    weights = [w_gate, w_up, swap(w_gate), swap(w_up)]
    downs = [w_down, swap(w_down)]
    arrived = [along_z(outgoing(j), j) for j in range(2)]
    piece = after(jnp.concatenate(arrived, axis=0), *weights[2:], downs[1])

    lines = [(y + o + 4) % 4 for o in OFFSETS]
    at = lambda d: jnp.where(d == 0, 0, jnp.where(d == 3, 1, d + 1))
    blocks = [
        [4 * at((v - y + 4) % 4) + r for r in range(4) for v in range(4)],
        [4 * r + at((8 - v - y) % 4) for r in range(4) for v in range(4)],
    ]
    here = [jnp.where(c == 0, p, q) for p, q in zip(*blocks)]
    there = [jnp.where(c == 0, q, p) for p, q in zip(*blocks)]
    scalars = jnp.stack(here + lines + [c] + [jnp.int32(0)] * 3 + there).astype(jnp.int32)

    low = jnp.concatenate([piece, plane(piece, 0, 1)], axis=0)
    high = jnp.concatenate([plane(piece, 0, -1), plane(piece, 0, 2)], axis=0)
    below_low, above_high = plane(low, 1, 1), plane(high, 1, -1)
    below_high, above_low = plane(high, 1, 1), plane(low, 1, -1)
    own_sums = gate_up([low, high], (0, 2), weights, scalars)
    far = [plane(after(below_low, own_sums), 1, 1), plane(above_high, 1, -1)]
    near_sums = gate_up([below_low, above_high], (0, 2), weights, scalars)
    sums = gate_up(
        [below_high, above_low, *far],
        (6, 8, 12, 14),
        weights,
        scalars,
        [own_sums, near_sums],
        ((0, 0, 0), (0, 2, 2), (1, 0, 4), (1, 2, 10)),
    )
    hidden, far_a, far_b = hidden_of(sums, swap(sums), *downs, scalars)
    below_a, below_b, above_a, above_b, own = down_of(hidden, *downs, scalars)

    from_below, from_above = plane(far_a, 0, 1), plane(far_b, 0, -1)
    got_high, got_low = plane(above_b, 0, 1), plane(below_a, 0, -1)
    to_above = [add(above_a[i], from_below[i]) for i in range(2)]
    to_below = [add(below_b[i], from_above[i]) for i in range(2)]
    got_1, got_2 = plane(to_above[1], 0, 1), plane(to_below[0], 0, -1)
    got_0, got_3 = plane(to_above[0], 0, 1), plane(to_below[1], 0, -1)
    mid_1, mid_2 = mid_sums(own, got_high, got_low, got_1, got_2)
    end_1, end_2 = plane(mid_1, 1, -1), plane(mid_2, 1, 1)
    mid_0, mid_3 = add(own[0], got_low[0], got_0), add(own[3], got_high[1], got_3)
    ends = [mid_0, end_1, end_2, plane(mid_3, 1, 2)]
    places = jnp.stack([(z - step + 8) % 8 for pair in ROUTES for step in pair]).astype(jnp.int32)
    table = lax.all_to_all(last_sum(places, ends), "expert", 0, 0, tiled=True)
    table = table.reshape(E * CAP, part)

    share = jax.nn.sigmoid(logits - logits[:, ::-1])
    hit = jnp.arange(E * CAP, dtype=jnp.int32)[None, :, None] == target[:, None, :]
    mix = jnp.sum(jnp.where(hit, share[:, None, :], 0.0), axis=2)
    high_mix = mix.astype(BF)
    low_mix = (mix - high_mix.astype(F32)).astype(BF)
    return (dot(high_mix, table) + dot(low_mix, table)).astype(BF)


def solution(mesh):
    grid = Mesh(mesh.devices.reshape(4, 8, 4, 2), ("dp", "expert", "ty", "core"))
    tensor = ("ty", "core")
    placed = (
        P(("dp", "expert"), None),
        P(("dp", "expert"), None),
        P(("dp", "expert"), None),
        P("expert", None, ("dp",) + tensor),
        P("expert", None, ("dp",) + tensor),
        P("expert", ("dp",) + tensor, None),
    )
    return jax.shard_map(
        body, mesh=grid, in_specs=placed, out_specs=P(("dp", "expert"), tensor), check_vma=False
    )
```

```python
import functools

import jax
import jax.numpy as jnp
import numpy as np
from jax import lax
from jax.experimental import pallas as pl
from jax.experimental.pallas import tpu as pltpu
from jax.sharding import Mesh, PartitionSpec as P

E = 8
CAP = 40
BF = jnp.bfloat16
F32 = jnp.float32
OFFSETS = (0, -1, 1, 2)
ROUTES = ((0, 4), (1, -1), (2, -2), (3, -3))
MIB = 2**20
VMEM = pl.BlockSpec(memory_space=pltpu.VMEM)
SMEM = pl.BlockSpec(memory_space=pltpu.SMEM)
ANY = pl.BlockSpec(memory_space=pl.ANY)
HBM = pl.BlockSpec(memory_space=pltpu.HBM)
COST = pl.CostEstimate(flops=MIB, bytes_accessed=MIB, transcendentals=0)


def dot(p, q):
    return jnp.dot(p, q, preferred_element_type=F32)


def add(*values):
    return sum(v.astype(F32) for v in values).astype(BF)


def plane(value, phase, step):
    pairs = []
    for x in range(4):
        for y in range(4):
            for c in range(2):
                along_x = (c == 0) == (phase == 0)
                to = ((x + step) % 4, y) if along_x else (x, (y + step) % 4)
                pairs.append(((x * 4 + y) * 2 + c, (to[0] * 4 + to[1]) * 2 + c))
    return lax.ppermute(value, ("dp", "ty", "core"), pairs)


def along_z(value, j):
    pairs = []
    for z in range(8):
        for y in range(4):
            for c in range(2):
                to = (z + ROUTES[-y % 4 if c else y][j]) % 8
                pairs.append(((z * 4 + y) * 2 + c, (to * 4 + y) * 2 + c))
    return lax.ppermute(value, ("expert", "ty", "core"), pairs)


def swap(value):
    return lax.ppermute(value, "core", [(0, 1), (1, 0)])


def after(value, *others):
    return pl.pallas_call(
        lambda *refs: None,
        in_specs=[ANY] * (1 + len(others)),
        out_specs=ANY,
        out_shape=jax.ShapeDtypeStruct(value.shape, value.dtype),
        input_output_aliases={0: 0},
        compiler_params=pltpu.CompilerParams(vmem_limit_bytes=MIB),
        cost_estimate=COST,
    )(value, *others)


def gate_up_kernel(places, merges, scalars, *refs):
    pieces = len(places)
    rows, weights, before = refs[:pieces], refs[pieces : pieces + 4], refs[pieces + 4 : -6]
    out, held, weight, row_sems, sems, merge_sems = refs[-6:]
    depth, step = weight.shape[1:]
    block = out.shape[1]
    start = pl.multiple_of(scalars[20] * depth, depth)
    at, row_copies, order = 0, [], []
    for i, (ref, place) in enumerate(zip(rows, places)):
        count = ref.shape[0]
        row_copies.append(pltpu.make_async_copy(ref, held.at[pl.ds(at, count)], row_sems.at[i]))
        at += count
        order += range(place, place + count // block)
    copies = [
        pltpu.make_async_copy(ref.at[pl.ds(start, depth)], weight.at[i], sems.at[i])
        for i, ref in enumerate(weights)
    ]
    merge_copies = [
        pltpu.make_async_copy(
            before[n].at[pl.ds(first, 2)], out.at[pl.ds(to, 2)], merge_sems.at[i]
        )
        for i, (n, first, to) in enumerate(merges)
    ]
    for copy in row_copies + copies + merge_copies:
        copy.start()
    for copy in row_copies:
        copy.wait()

    @pl.loop(0, 4)
    def _(n):
        pltpu.make_async_copy(weights[0].at[pl.ds(start, depth)], weight.at[n], sems.at[n]).wait()
        value = dot(held[...], weight[n])
        column = pl.multiple_of(n * step, step)
        for i, place in enumerate(order):
            out[place, :, pl.ds(column, step)] = value[i * block : (i + 1) * block].astype(BF)

    for copy in merge_copies:
        copy.wait()


def gate_up(rows, places, weights, scalars, before=(), merges=()):
    count, block = sum(r.shape[0] for r in rows), 2 * CAP
    depth, step = weights[0].shape
    depth //= 2
    blocks = count // block + 2 * len(merges)
    return pl.pallas_call(
        functools.partial(gate_up_kernel, places, merges),
        in_specs=[SMEM] + [ANY] * len(rows) + [HBM] * 4 + [ANY] * len(before),
        out_specs=VMEM,
        out_shape=jax.ShapeDtypeStruct((blocks, block, 4 * step), BF),
        scratch_shapes=[
            pltpu.VMEM((count, depth), BF),
            pltpu.VMEM((4, depth, step), BF),
            pltpu.SemaphoreType.DMA((len(rows),)),
            pltpu.SemaphoreType.DMA((4,)),
            pltpu.SemaphoreType.DMA((max(len(merges), 1),)),
        ],
        compiler_params=pltpu.CompilerParams(vmem_limit_bytes=20 * MIB),
        cost_estimate=COST,
    )(scalars, *rows, *weights, *before)


def down_copies(scalars, mine, theirs, down, sems, count=4):
    units, part = mine.shape[0], down.shape[2]
    copies = []
    for k in range(count):
        start = pl.multiple_of((2 * scalars[16 + k] + scalars[20]) * part, part)
        for side, ref in enumerate((mine, theirs)):
            copies.append(
                pltpu.make_async_copy(
                    ref.at[:, pl.ds(start, part)],
                    down.at[k, pl.ds(side * units, units)],
                    sems.at[2 * k + side],
                )
            )
    return copies


def hidden_kernel(
    scalars, sums, got, mine, theirs, hidden, far_a, far_b, down, sems
):
    copies = down_copies(scalars, mine, theirs, down, sems)
    for copy in copies:
        copy.start()
    units = hidden.shape[1] // 2
    rows = hidden.shape[0] // 4
    block = rows // 4
    for i in range(16):
        here, there = sums[scalars[i]].astype(F32), got[scalars[24 + i]].astype(F32)
        for side in range(2):
            at, other = 2 * units * side, 2 * units * (1 - side)
            gate = here[:, at : at + units] + there[:, other : other + units]
            upper = here[:, at + units : at + 2 * units]
            upper = upper + there[:, other + units : other + 2 * units]
            value = gate / (1.0 + jnp.exp(-gate)) * upper
            hidden[i * block : (i + 1) * block, side * units : (side + 1) * units] = value.astype(BF)
    outs = (far_a.at[0], far_a.at[1], far_b.at[0], far_b.at[1])
    for copy in copies:
        copy.wait()

    @pl.when(scalars[20] == 0)
    def _():
        for k in range(4):
            outs[k][...] = dot(hidden[3 * rows :, :], down[k]).astype(BF)

    @pl.when(scalars[20] == 1)
    def _():
        value = dot(hidden[...], down[3]).astype(BF)
        for r in range(4):
            outs[r][...] = value[r * rows : (r + 1) * rows]


def hidden_of(sums, got, mine, theirs, scalars):
    rows, units = sums.shape[0] * sums.shape[1], 2 * mine.shape[0]
    part = mine.shape[1] // 8
    piece = jax.ShapeDtypeStruct((2, rows // 4, part), BF)
    return pl.pallas_call(
        hidden_kernel,
        in_specs=[SMEM] + [VMEM] * 2 + [HBM] * 2,
        out_specs=[VMEM] * 3,
        out_shape=[jax.ShapeDtypeStruct((rows, units), BF), piece, piece],
        scratch_shapes=[pltpu.VMEM((4, units, part), BF), pltpu.SemaphoreType.DMA((8,))],
        compiler_params=pltpu.CompilerParams(vmem_limit_bytes=20 * MIB),
        cost_estimate=COST,
    )(scalars, sums, got, mine, theirs)


def down_kernel(
    scalars, hidden, mine, theirs, below_a, below_b, above_a, above_b, own, down, sems
):
    copies = down_copies(scalars, mine, theirs, down, sems)
    for copy in copies:
        copy.start()
    for copy in copies:
        copy.wait()
    rows = hidden.shape[0] // 4
    outs = (
        (own.at[0], own.at[1], own.at[2], own.at[3]),
        (below_a.at[0], below_a.at[1], below_b.at[0], below_b.at[1]),
        (above_a.at[0], above_a.at[1], above_b.at[0], above_b.at[1]),
    )

    @pl.when(scalars[20] == 0)
    def _():
        for k in range(4):
            value = dot(hidden[: 3 * rows, :], down[k]).astype(BF)
            for r in range(3):
                outs[r][k][...] = value[r * rows : (r + 1) * rows]

    @pl.when(scalars[20] == 1)
    def _():
        for k in range(3):
            value = dot(hidden[...], down[k]).astype(BF)
            for r in range(4):
                outs[k][r][...] = value[r * rows : (r + 1) * rows]


def down_of(hidden, mine, theirs, scalars):
    rows, units = hidden.shape
    part = mine.shape[1] // 8
    return pl.pallas_call(
        down_kernel,
        in_specs=[SMEM, VMEM, HBM, HBM],
        out_specs=[VMEM] * 5,
        out_shape=[jax.ShapeDtypeStruct((s, rows // 4, part), BF) for s in (2, 2, 2, 2, 4)],
        scratch_shapes=[pltpu.VMEM((4, units, part), BF), pltpu.SemaphoreType.DMA((8,))],
        compiler_params=pltpu.CompilerParams(vmem_limit_bytes=20 * MIB),
        cost_estimate=COST,
    )(scalars, hidden, mine, theirs)


def mid_kernel(own, high, low, got_1, got_3, mid_1, mid_3):
    for i, parts, out in ((1, (low.at[1], got_1), mid_1), (3, (high.at[1], got_3), mid_3)):
        total = own[i].astype(F32)
        for part in parts:
            total = total + part[...].astype(F32)
        out[...] = total.astype(BF)


def mid_sums(*values):
    piece = jax.ShapeDtypeStruct(values[-1].shape, BF)
    return pl.pallas_call(
        mid_kernel,
        in_specs=[VMEM] * 5,
        out_specs=[VMEM] * 2,
        out_shape=[piece, piece],
        compiler_params=pltpu.CompilerParams(vmem_limit_bytes=16 * MIB),
        cost_estimate=COST,
    )(*values)


def last_kernel(places, a, b, c, d, out):
    for i in range(E):
        total = a[i].astype(F32) + b[i].astype(F32) + c[i].astype(F32) + d[i].astype(F32)
        out[places[i]] = total.astype(BF)


def last_sum(places, parts):
    shape = (E, CAP, parts[0].shape[1])
    return pl.pallas_call(
        last_kernel,
        in_specs=[SMEM] + [VMEM] * 4,
        out_specs=VMEM,
        out_shape=jax.ShapeDtypeStruct(shape, BF),
        compiler_params=pltpu.CompilerParams(vmem_limit_bytes=16 * MIB),
        cost_estimate=COST,
    )(places, *[p.reshape(shape) for p in parts])


def body(tokens, routes, logits, w_gate, w_up, w_down):
    rows, width = tokens.shape
    half = width // 2
    part = half // 4
    y, c, z = lax.axis_index("ty"), lax.axis_index("core"), lax.axis_index("expert")

    ids = jnp.arange(E, dtype=jnp.int32)[:, None]
    named = (routes[:, 0][None, :] == ids) | (routes[:, 1][None, :] == ids)
    numbers = jnp.arange(rows, dtype=jnp.int32)
    earlier = (numbers[:, None] < numbers[None, :]).astype(BF)
    before = dot(named.astype(BF), earlier)
    columns = lax.dynamic_slice_in_dim(tokens, c * half, half, 1)
    slots = jnp.arange(CAP, dtype=jnp.int32).astype(F32)
    line = jnp.where(c == 0, y, -y % 4)

    def outgoing(j):
        step = jnp.int32(ROUTES[0][j])
        for number in range(1, 4):
            step = jnp.where(line == number, ROUTES[number][j], step)
        expert = (z + step + 8) % 8
        row = lambda v: lax.dynamic_slice_in_dim(v, expert, 1, 0)
        hit = row(named) & (row(before) == slots[:, None])
        return dot(hit.astype(BF), columns).astype(BF)

    w_gate, w_up, w_down = w_gate[0], w_up[0], w_down[0]
    weights = [w_gate, w_up, swap(w_gate), swap(w_up)]
    downs = [w_down, swap(w_down)]
    arrived = [along_z(outgoing(j), j) for j in range(2)]
    piece = after(jnp.concatenate(arrived, axis=0), *weights[2:], downs[1])

    lines = [(y + o + 4) % 4 for o in OFFSETS]
    at = lambda d: jnp.where(d == 0, 0, jnp.where(d == 3, 1, d + 1))
    blocks = [
        [4 * at((v - y + 4) % 4) + r for r in range(4) for v in range(4)],
        [4 * r + at((8 - v - y) % 4) for r in range(4) for v in range(4)],
    ]
    here = [jnp.where(c == 0, p, q) for p, q in zip(*blocks)]
    there = [jnp.where(c == 0, q, p) for p, q in zip(*blocks)]
    scalars = jnp.stack(here + lines + [c] + [jnp.int32(0)] * 3 + there).astype(jnp.int32)

    low = jnp.concatenate([piece, plane(piece, 0, 1)], axis=0)
    high = jnp.concatenate([plane(piece, 0, -1), plane(piece, 0, 2)], axis=0)
    below_low, above_low = plane(low, 1, 1), plane(low, 1, -1)
    below_high, above_high = plane(high, 1, 1), plane(high, 1, -1)
    own_sums = gate_up([low, high], (0, 2), weights, scalars)
    far = [plane(after(below_low, own_sums), 1, 1), plane(above_high, 1, -1)]
    near_sums = gate_up([below_low, above_low], (0, 2), weights, scalars)
    sums = gate_up(
        [below_high, above_high, *far],
        (6, 10, 12, 14),
        weights,
        scalars,
        [own_sums, near_sums],
        ((0, 0, 0), (0, 2, 2), (1, 0, 4), (1, 2, 8)),
    )
    hidden, far_a, far_b = hidden_of(sums, swap(sums), *downs, scalars)
    below_a, below_b, above_a, above_b, own = down_of(hidden, *downs, scalars)

    from_below, from_above = plane(far_a, 0, 1), plane(far_b, 0, -1)
    got_high, got_low = plane(above_b, 0, 1), plane(below_a, 0, -1)
    to_above = [add(above_a[i], from_below[i]) for i in range(2)]
    to_below = [add(below_b[i], from_above[i]) for i in range(2)]
    got_1, got_3 = plane(to_above[1], 0, 1), plane(to_below[1], 0, -1)
    got_0, got_2 = plane(to_above[0], 0, 1), plane(to_below[0], 0, -1)
    mid_1, mid_3 = mid_sums(own, got_high, got_low, got_1, got_3)
    end_3, end_1 = plane(mid_3, 1, 2), plane(mid_1, 1, -1)
    mid_0, mid_2 = add(own[0], got_low[0], got_0), add(own[2], got_high[0], got_2)
    ends = [mid_0, end_1, plane(mid_2, 1, 1), end_3]
    places = jnp.stack([(z - step + 8) % 8 for pair in ROUTES for step in pair]).astype(jnp.int32)
    table = lax.all_to_all(last_sum(places, ends), "expert", 0, 0, tiled=True)
    table = table.reshape(E * CAP, part)

    share = jax.nn.sigmoid(logits - logits[:, ::-1])
    shares = [jnp.where(routes[:, k][None, :] == ids, share[:, k][None, :], 0.0) for k in range(2)]
    hit = named[:, None, :] & (before[:, None, :] == slots[None, :, None])
    mix = jnp.where(hit, (shares[0] + shares[1])[:, None, :], 0.0).reshape(E * CAP, rows)
    high_mix = mix.astype(BF)
    low_mix = (mix - high_mix.astype(F32)).astype(BF)
    back = lambda m: lax.dot_general(m, table, (((0,), (0,)), ((), ())), preferred_element_type=F32)
    return (back(high_mix) + back(low_mix)).astype(BF)


def solution(mesh):
    grid = Mesh(mesh.devices.reshape(4, 8, 4, 2), ("dp", "expert", "ty", "core"))
    tensor = ("ty", "core")
    placed = (
        P(("dp", "expert"), None),
        P(("dp", "expert"), None),
        P(("dp", "expert"), None),
        P("expert", None, ("dp",) + tensor),
        P("expert", None, ("dp",) + tensor),
        P("expert", ("dp",) + tensor, None),
    )
    return jax.shard_map(
        body, mesh=grid, in_specs=placed, out_specs=P(("dp", "expert"), tensor), check_vma=False
    )
```

```python
import functools

import jax
import jax.numpy as jnp
import numpy as np
from jax import lax
from jax.experimental import pallas as pl
from jax.experimental.pallas import tpu as pltpu
from jax.sharding import Mesh, PartitionSpec as P

E = 8
CAP = 40
BF = jnp.bfloat16
F32 = jnp.float32
OFFSETS = (0, -1, 1, 2)
ROUTES = ((0, 4), (1, -1), (2, -2), (3, -3))
MIB = 2**20
VMEM = pl.BlockSpec(memory_space=pltpu.VMEM)
ANY = pl.BlockSpec(memory_space=pl.ANY)
HBM = pl.BlockSpec(memory_space=pltpu.HBM)
COST = pl.CostEstimate(flops=MIB, bytes_accessed=MIB, transcendentals=0)


def dot(p, q):
    return jnp.dot(p, q, preferred_element_type=F32)


def add(*values):
    return sum(v.astype(F32) for v in values).astype(BF)


def plane(value, phase, step):
    pairs = []
    for x in range(4):
        for y in range(4):
            for c in range(2):
                along_x = (c == 0) == (phase == 0)
                to = ((x + step) % 4, y) if along_x else (x, (y + step) % 4)
                pairs.append(((x * 4 + y) * 2 + c, (to[0] * 4 + to[1]) * 2 + c))
    return lax.ppermute(value, ("dp", "ty", "core"), pairs)


def along_z(value, j):
    pairs = []
    for z in range(8):
        for y in range(4):
            for c in range(2):
                to = (z + ROUTES[-y % 4 if c else y][j]) % 8
                pairs.append(((z * 4 + y) * 2 + c, (to * 4 + y) * 2 + c))
    return lax.ppermute(value, ("expert", "ty", "core"), pairs)


def swap(value):
    return lax.ppermute(value, "core", [(0, 1), (1, 0)])


def after(value, *others):
    return pl.pallas_call(
        lambda *refs: None,
        in_specs=[ANY] * (1 + len(others)),
        out_specs=ANY,
        out_shape=jax.ShapeDtypeStruct(value.shape, value.dtype),
        input_output_aliases={0: 0},
        compiler_params=pltpu.CompilerParams(vmem_limit_bytes=MIB),
        cost_estimate=COST,
    )(value, *others)


def gate_up_kernel(places, merges, *refs):
    pieces = len(places)
    rows, weights, before = refs[:pieces], refs[pieces : pieces + 4], refs[pieces + 4 : -6]
    out, held, weight, row_sems, sems, merge_sems = refs[-6:]
    depth, step = weight.shape[1:]
    block = out.shape[1]
    start = pl.multiple_of(lax.axis_index("core") * depth, depth)
    at, row_copies, order = 0, [], []
    for i, (ref, place) in enumerate(zip(rows, places)):
        count = ref.shape[0]
        row_copies.append(pltpu.make_async_copy(ref, held.at[pl.ds(at, count)], row_sems.at[i]))
        at += count
        order += range(place, place + count // block)
    copies = [
        pltpu.make_async_copy(ref.at[pl.ds(start, depth)], weight.at[i], sems.at[i])
        for i, ref in enumerate(weights)
    ]
    merge_copies = [
        pltpu.make_async_copy(
            before[n].at[pl.ds(first, 2)], out.at[pl.ds(to, 2)], merge_sems.at[i]
        )
        for i, (n, first, to) in enumerate(merges)
    ]
    for copy in row_copies + copies + merge_copies:
        copy.start()
    for copy in row_copies:
        copy.wait()

    @pl.loop(0, 4)
    def _(n):
        pltpu.make_async_copy(weights[0].at[pl.ds(start, depth)], weight.at[n], sems.at[n]).wait()
        value = dot(held[...], weight[n])
        column = pl.multiple_of(n * step, step)
        for i, place in enumerate(order):
            out[place, :, pl.ds(column, step)] = value[i * block : (i + 1) * block].astype(BF)

    for copy in merge_copies:
        copy.wait()


def gate_up(rows, places, weights, before=(), merges=()):
    count, block = sum(r.shape[0] for r in rows), 2 * CAP
    depth, step = weights[0].shape
    depth //= 2
    blocks = count // block + 2 * len(merges)
    return pl.pallas_call(
        functools.partial(gate_up_kernel, places, merges),
        in_specs=[ANY] * len(rows) + [HBM] * 4 + [ANY] * len(before),
        out_specs=VMEM,
        out_shape=jax.ShapeDtypeStruct((blocks, block, 4 * step), BF),
        scratch_shapes=[
            pltpu.VMEM((count, depth), BF),
            pltpu.VMEM((4, depth, step), BF),
            pltpu.SemaphoreType.DMA((len(rows),)),
            pltpu.SemaphoreType.DMA((4,)),
            pltpu.SemaphoreType.DMA((max(len(merges), 1),)),
        ],
        compiler_params=pltpu.CompilerParams(vmem_limit_bytes=20 * MIB),
        cost_estimate=COST,
    )(*rows, *weights, *before)


def line_at(offset, y):
    return (y + offset + 4) & 3


def block_at(core, y, r, v):
    place = lambda d: jnp.where(d == 0, 0, jnp.where(d == 3, 1, d + 1))
    first = 4 * place((v - y + 4) & 3) + r
    return jnp.where(core == 0, first, 4 * r + place((8 - v - y) & 3))


def down_copies(mine, theirs, down, sems, count=4):
    units, part = mine.shape[0], down.shape[2]
    y, core = lax.axis_index("ty"), lax.axis_index("core")
    copies = []
    for k in range(count):
        start = pl.multiple_of((2 * line_at(OFFSETS[k], y) + core) * part, part)
        for side, ref in enumerate((mine, theirs)):
            copies.append(
                pltpu.make_async_copy(
                    ref.at[:, pl.ds(start, part)],
                    down.at[k, pl.ds(side * units, units)],
                    sems.at[2 * k + side],
                )
            )
    return copies


def hidden_kernel(
    sums, got, mine, theirs, hidden, far_a, far_b, down, sems
):
    copies = down_copies(mine, theirs, down, sems)
    for copy in copies:
        copy.start()
    units = hidden.shape[1] // 2
    rows = hidden.shape[0] // 4
    block = rows // 4
    y, core = lax.axis_index("ty"), lax.axis_index("core")
    for i in range(16):
        here = sums[block_at(core, y, i // 4, i % 4)].astype(F32)
        there = got[block_at(1 - core, y, i // 4, i % 4)].astype(F32)
        for side in range(2):
            at, other = 2 * units * side, 2 * units * (1 - side)
            gate = here[:, at : at + units] + there[:, other : other + units]
            upper = here[:, at + units : at + 2 * units]
            upper = upper + there[:, other + units : other + 2 * units]
            value = gate / (1.0 + jnp.exp(-gate)) * upper
            hidden[i * block : (i + 1) * block, side * units : (side + 1) * units] = value.astype(BF)
    outs = (far_a.at[0], far_a.at[1], far_b.at[0], far_b.at[1])
    for copy in copies:
        copy.wait()

    @pl.when(lax.axis_index("core") == 0)
    def _():
        for k in range(4):
            outs[k][...] = dot(hidden[3 * rows :, :], down[k]).astype(BF)

    @pl.when(lax.axis_index("core") == 1)
    def _():
        value = dot(hidden[...], down[3]).astype(BF)
        for r in range(4):
            outs[r][...] = value[r * rows : (r + 1) * rows]


def hidden_of(sums, got, mine, theirs):
    rows, units = sums.shape[0] * sums.shape[1], 2 * mine.shape[0]
    part = mine.shape[1] // 8
    piece = jax.ShapeDtypeStruct((2, rows // 4, part), BF)
    return pl.pallas_call(
        hidden_kernel,
        in_specs=[VMEM] * 2 + [HBM] * 2,
        out_specs=[VMEM] * 3,
        out_shape=[jax.ShapeDtypeStruct((rows, units), BF), piece, piece],
        scratch_shapes=[pltpu.VMEM((4, units, part), BF), pltpu.SemaphoreType.DMA((8,))],
        compiler_params=pltpu.CompilerParams(vmem_limit_bytes=20 * MIB),
        cost_estimate=COST,
    )(sums, got, mine, theirs)


def down_kernel(
    hidden, mine, theirs, below_a, below_b, above_a, above_b, own, down, sems
):
    copies = down_copies(mine, theirs, down, sems)
    for copy in copies:
        copy.start()
    for copy in copies:
        copy.wait()
    rows = hidden.shape[0] // 4
    outs = (
        (own.at[0], own.at[1], own.at[2], own.at[3]),
        (below_a.at[0], below_a.at[1], below_b.at[0], below_b.at[1]),
        (above_a.at[0], above_a.at[1], above_b.at[0], above_b.at[1]),
    )

    @pl.when(lax.axis_index("core") == 0)
    def _():
        for k in range(4):
            value = dot(hidden[: 3 * rows, :], down[k]).astype(BF)
            for r in range(3):
                outs[r][k][...] = value[r * rows : (r + 1) * rows]

    @pl.when(lax.axis_index("core") == 1)
    def _():
        for k in range(3):
            value = dot(hidden[...], down[k]).astype(BF)
            for r in range(4):
                outs[k][r][...] = value[r * rows : (r + 1) * rows]


def down_of(hidden, mine, theirs):
    rows, units = hidden.shape
    part = mine.shape[1] // 8
    return pl.pallas_call(
        down_kernel,
        in_specs=[VMEM, HBM, HBM],
        out_specs=[VMEM] * 5,
        out_shape=[jax.ShapeDtypeStruct((s, rows // 4, part), BF) for s in (2, 2, 2, 2, 4)],
        scratch_shapes=[pltpu.VMEM((4, units, part), BF), pltpu.SemaphoreType.DMA((8,))],
        compiler_params=pltpu.CompilerParams(vmem_limit_bytes=20 * MIB),
        cost_estimate=COST,
    )(hidden, mine, theirs)


def mid_kernel(own, high, low, got_1, got_3, mid_1, mid_3):
    for i, parts, out in ((1, (low.at[1], got_1), mid_1), (3, (high.at[1], got_3), mid_3)):
        total = own[i].astype(F32)
        for part in parts:
            total = total + part[...].astype(F32)
        out[...] = total.astype(BF)


def mid_sums(*values):
    piece = jax.ShapeDtypeStruct(values[-1].shape, BF)
    return pl.pallas_call(
        mid_kernel,
        in_specs=[VMEM] * 5,
        out_specs=[VMEM] * 2,
        out_shape=[piece, piece],
        compiler_params=pltpu.CompilerParams(vmem_limit_bytes=16 * MIB),
        cost_estimate=COST,
    )(*values)


def last_kernel(a, b, c, d, out):
    z = lax.axis_index("expert")
    for i, step in enumerate(sum(ROUTES, ())):
        total = a[i].astype(F32) + b[i].astype(F32) + c[i].astype(F32) + d[i].astype(F32)
        out[(z - step + 8) & 7] = total.astype(BF)


def last_sum(parts):
    shape = (E, CAP, parts[0].shape[1])
    return pl.pallas_call(
        last_kernel,
        in_specs=[VMEM] * 4,
        out_specs=VMEM,
        out_shape=jax.ShapeDtypeStruct(shape, BF),
        compiler_params=pltpu.CompilerParams(vmem_limit_bytes=16 * MIB),
        cost_estimate=COST,
    )(*[p.reshape(shape) for p in parts])


def body(tokens, routes, logits, w_gate, w_up, w_down):
    rows, width = tokens.shape
    half = width // 2
    part = half // 4
    y, c, z = lax.axis_index("ty"), lax.axis_index("core"), lax.axis_index("expert")

    ids = jnp.arange(E, dtype=jnp.int32)[:, None]
    named = (routes[:, 0][None, :] == ids) | (routes[:, 1][None, :] == ids)
    numbers = jnp.arange(rows, dtype=jnp.int32)
    earlier = (numbers[:, None] < numbers[None, :]).astype(BF)
    before = dot(named.astype(BF), earlier)
    columns = lax.dynamic_slice_in_dim(tokens, c * half, half, 1)
    slots = jnp.arange(CAP, dtype=jnp.int32).astype(F32)
    line = jnp.where(c == 0, y, -y % 4)

    def outgoing(j):
        step = jnp.int32(ROUTES[0][j])
        for number in range(1, 4):
            step = jnp.where(line == number, ROUTES[number][j], step)
        expert = (z + step + 8) % 8
        row = lambda v: lax.dynamic_slice_in_dim(v, expert, 1, 0)
        hit = row(named) & (row(before) == slots[:, None])
        return dot(hit.astype(BF), columns).astype(BF)

    w_gate, w_up, w_down = w_gate[0], w_up[0], w_down[0]
    weights = [w_gate, w_up, swap(w_gate), swap(w_up)]
    downs = [w_down, swap(w_down)]
    arrived = [along_z(outgoing(j), j) for j in range(2)]
    piece = after(jnp.concatenate(arrived, axis=0), *weights[2:], downs[1])

    low = jnp.concatenate([piece, plane(piece, 0, 1)], axis=0)
    high = jnp.concatenate([plane(piece, 0, -1), plane(piece, 0, 2)], axis=0)
    below_low, above_low = plane(low, 1, 1), plane(low, 1, -1)
    below_high, above_high = plane(high, 1, 1), plane(high, 1, -1)
    own_sums = gate_up([low, high], (0, 2), weights)
    far = [plane(after(below_low, own_sums), 1, 1), plane(above_high, 1, -1)]
    near_sums = gate_up([below_low, above_low], (0, 2), weights)
    sums = gate_up(
        [below_high, above_high, *far],
        (6, 10, 12, 14),
        weights,
        [own_sums, near_sums],
        ((0, 0, 0), (0, 2, 2), (1, 0, 4), (1, 2, 8)),
    )
    hidden, far_a, far_b = hidden_of(sums, swap(sums), *downs)
    below_a, below_b, above_a, above_b, own = down_of(hidden, *downs)

    from_below, from_above = plane(far_a, 0, 1), plane(far_b, 0, -1)
    got_high, got_low = plane(above_b, 0, 1), plane(below_a, 0, -1)
    to_above = [add(above_a[i], from_below[i]) for i in range(2)]
    to_below = [add(below_b[i], from_above[i]) for i in range(2)]
    got_1, got_3 = plane(to_above[1], 0, 1), plane(to_below[1], 0, -1)
    got_0, got_2 = plane(to_above[0], 0, 1), plane(to_below[0], 0, -1)
    mid_1, mid_3 = mid_sums(own, got_high, got_low, got_1, got_3)
    end_3, end_1 = plane(mid_3, 1, 2), plane(mid_1, 1, -1)
    mid_0, mid_2 = add(own[0], got_low[0], got_0), add(own[2], got_high[0], got_2)
    ends = [mid_0, end_1, plane(mid_2, 1, 1), end_3]
    table = lax.all_to_all(last_sum(ends), "expert", 0, 0, tiled=True)
    table = table.reshape(E * CAP, part)

    share = jax.nn.sigmoid(logits - logits[:, ::-1])
    shares = [jnp.where(routes[:, k][None, :] == ids, share[:, k][None, :], 0.0) for k in range(2)]
    hit = named[:, None, :] & (before[:, None, :] == slots[None, :, None])
    mix = jnp.where(hit, (shares[0] + shares[1])[:, None, :], 0.0).reshape(E * CAP, rows)
    high_mix = mix.astype(BF)
    low_mix = (mix - high_mix.astype(F32)).astype(BF)
    back = lambda m: lax.dot_general(m, table, (((0,), (0,)), ((), ())), preferred_element_type=F32)
    return (back(high_mix) + back(low_mix)).astype(BF)


def solution(mesh):
    grid = Mesh(mesh.devices.reshape(4, 8, 4, 2), ("dp", "expert", "ty", "core"))
    tensor = ("ty", "core")
    placed = (
        P(("dp", "expert"), None),
        P(("dp", "expert"), None),
        P(("dp", "expert"), None),
        P("expert", None, ("dp",) + tensor),
        P("expert", None, ("dp",) + tensor),
        P("expert", ("dp",) + tensor, None),
    )
    return jax.shard_map(
        body, mesh=grid, in_specs=placed, out_specs=P(("dp", "expert"), tensor), check_vma=False
    )
```

```python
import functools

import jax
import jax.numpy as jnp
import numpy as np
from jax import lax
from jax.experimental import pallas as pl
from jax.experimental.pallas import tpu as pltpu
from jax.sharding import Mesh, PartitionSpec as P

E = 8
CAP = 40
BF = jnp.bfloat16
F32 = jnp.float32
OFFSETS = (0, -1, 1, 2)
ROUTES = ((0, 4), (1, -1), (2, -2), (3, -3))
MIB = 2**20
VMEM = pl.BlockSpec(memory_space=pltpu.VMEM)
ANY = pl.BlockSpec(memory_space=pl.ANY)
HBM = pl.BlockSpec(memory_space=pltpu.HBM)
COST = pl.CostEstimate(flops=MIB, bytes_accessed=MIB, transcendentals=0)


def dot(p, q):
    return jnp.dot(p, q, preferred_element_type=F32)


def add(*values):
    return sum(v.astype(F32) for v in values).astype(BF)


def plane(value, phase, step):
    pairs = []
    for x in range(4):
        for y in range(4):
            for c in range(2):
                along_x = (c == 0) == (phase == 0)
                to = ((x + step) % 4, y) if along_x else (x, (y + step) % 4)
                pairs.append(((x * 4 + y) * 2 + c, (to[0] * 4 + to[1]) * 2 + c))
    return lax.ppermute(value, ("dp", "ty", "core"), pairs)


def along_z(value, j):
    pairs = []
    for z in range(8):
        for y in range(4):
            for c in range(2):
                to = (z + ROUTES[-y % 4 if c else y][j]) % 8
                pairs.append(((z * 4 + y) * 2 + c, (to * 4 + y) * 2 + c))
    return lax.ppermute(value, ("expert", "ty", "core"), pairs)


def swap(value):
    return lax.ppermute(value, "core", [(0, 1), (1, 0)])


def after(value, *others):
    return pl.pallas_call(
        lambda *refs: None,
        in_specs=[ANY] * (1 + len(others)),
        out_specs=ANY,
        out_shape=jax.ShapeDtypeStruct(value.shape, value.dtype),
        input_output_aliases={0: 0},
        compiler_params=pltpu.CompilerParams(vmem_limit_bytes=MIB),
        cost_estimate=COST,
    )(value, *others)


def gate_up_kernel(places, merges, *refs):
    pieces = len(places)
    rows, weights, before = refs[:pieces], refs[pieces : pieces + 4], refs[pieces + 4 : -6]
    out, held, weight, row_sems, sems, merge_sems = refs[-6:]
    depth, step = weight.shape[1:]
    block = out.shape[1]
    start = pl.multiple_of(lax.axis_index("core") * depth, depth)
    at, row_copies, order = 0, [], []
    for i, (ref, place) in enumerate(zip(rows, places)):
        count = ref.shape[0]
        row_copies.append(pltpu.make_async_copy(ref, held.at[pl.ds(at, count)], row_sems.at[i]))
        at += count
        order += range(place, place + count // block)
    copies = [
        pltpu.make_async_copy(ref.at[pl.ds(start, depth)], weight.at[i], sems.at[i])
        for i, ref in enumerate(weights)
    ]
    merge_copies = [
        pltpu.make_async_copy(
            before[n].at[pl.ds(first, 2)], out.at[pl.ds(to, 2)], merge_sems.at[i]
        )
        for i, (n, first, to) in enumerate(merges)
    ]
    for copy in row_copies + copies + merge_copies:
        copy.start()
    for copy in row_copies:
        copy.wait()

    @pl.loop(0, 4)
    def _(n):
        pltpu.make_async_copy(weights[0].at[pl.ds(start, depth)], weight.at[n], sems.at[n]).wait()
        value = dot(held[...], weight[n])
        column = pl.multiple_of(n * step, step)
        for i, place in enumerate(order):
            out[place, :, pl.ds(column, step)] = value[i * block : (i + 1) * block].astype(BF)

    for copy in merge_copies:
        copy.wait()


def gate_up(rows, places, weights, before=(), merges=()):
    count, block = sum(r.shape[0] for r in rows), 2 * CAP
    depth, step = weights[0].shape
    depth //= 2
    blocks = count // block + 2 * len(merges)
    return pl.pallas_call(
        functools.partial(gate_up_kernel, places, merges),
        in_specs=[ANY] * len(rows) + [HBM] * 4 + [ANY] * len(before),
        out_specs=VMEM,
        out_shape=jax.ShapeDtypeStruct((blocks, block, 4 * step), BF),
        scratch_shapes=[
            pltpu.VMEM((count, depth), BF),
            pltpu.VMEM((4, depth, step), BF),
            pltpu.SemaphoreType.DMA((len(rows),)),
            pltpu.SemaphoreType.DMA((4,)),
            pltpu.SemaphoreType.DMA((max(len(merges), 1),)),
        ],
        compiler_params=pltpu.CompilerParams(vmem_limit_bytes=20 * MIB),
        cost_estimate=COST,
    )(*rows, *weights, *before)


def line_at(offset, y):
    return (y + offset + 4) & 3


def block_at(core, y, r, v):
    place = lambda d: jnp.where(d == 0, 0, jnp.where(d == 3, 1, d + 1))
    first = 4 * place((v - y + 4) & 3) + r
    return jnp.where(core == 0, first, 4 * r + place((8 - v - y) & 3))


def down_copies(mine, theirs, down, sems, count=4):
    units, part = mine.shape[0], down.shape[2]
    y, core = lax.axis_index("ty"), lax.axis_index("core")
    copies = []
    for k in range(count):
        start = pl.multiple_of((2 * line_at(OFFSETS[k], y) + core) * part, part)
        for side, ref in enumerate((mine, theirs)):
            copies.append(
                pltpu.make_async_copy(
                    ref.at[:, pl.ds(start, part)],
                    down.at[k, pl.ds(side * units, units)],
                    sems.at[2 * k + side],
                )
            )
    return copies


def hidden_kernel(
    sums, got, mine, theirs, hidden, far_a, far_b, down, sems
):
    copies = down_copies(mine, theirs, down, sems)
    for copy in copies:
        copy.start()
    units = hidden.shape[1] // 2
    rows = hidden.shape[0] // 4
    block = rows // 4
    y, core = lax.axis_index("ty"), lax.axis_index("core")
    for i in range(16):
        here = sums[block_at(core, y, i // 4, i % 4)].astype(F32)
        there = got[block_at(1 - core, y, i // 4, i % 4)].astype(F32)
        for side in range(2):
            at, other = 2 * units * side, 2 * units * (1 - side)
            gate = here[:, at : at + units] + there[:, other : other + units]
            upper = here[:, at + units : at + 2 * units]
            upper = upper + there[:, other + units : other + 2 * units]
            value = gate / (1.0 + jnp.exp(-gate)) * upper
            hidden[i * block : (i + 1) * block, side * units : (side + 1) * units] = value.astype(BF)
    outs = (far_a.at[0], far_a.at[1], far_b.at[0], far_b.at[1])
    for copy in copies:
        copy.wait()

    @pl.when(lax.axis_index("core") == 0)
    def _():
        for k in range(4):
            outs[k][...] = dot(hidden[3 * rows :, :], down[k]).astype(BF)

    @pl.when(lax.axis_index("core") == 1)
    def _():
        value = dot(hidden[...], down[3]).astype(BF)
        for r in range(4):
            outs[r][...] = value[r * rows : (r + 1) * rows]


def hidden_of(sums, got, mine, theirs):
    rows, units = sums.shape[0] * sums.shape[1], 2 * mine.shape[0]
    part = mine.shape[1] // 8
    piece = jax.ShapeDtypeStruct((2, rows // 4, part), BF)
    return pl.pallas_call(
        hidden_kernel,
        in_specs=[VMEM] * 2 + [HBM] * 2,
        out_specs=[VMEM] * 3,
        out_shape=[jax.ShapeDtypeStruct((rows, units), BF), piece, piece],
        scratch_shapes=[pltpu.VMEM((4, units, part), BF), pltpu.SemaphoreType.DMA((8,))],
        compiler_params=pltpu.CompilerParams(vmem_limit_bytes=20 * MIB),
        cost_estimate=COST,
    )(sums, got, mine, theirs)


def down_kernel(
    hidden, mine, theirs, below_a, below_b, above_a, above_b, own, down, sems
):
    copies = down_copies(mine, theirs, down, sems)
    for copy in copies:
        copy.start()
    for copy in copies:
        copy.wait()
    rows = hidden.shape[0] // 4
    outs = (
        (own.at[0], own.at[1], own.at[2], own.at[3]),
        (below_a.at[0], below_a.at[1], below_b.at[0], below_b.at[1]),
        (above_a.at[0], above_a.at[1], above_b.at[0], above_b.at[1]),
    )

    @pl.when(lax.axis_index("core") == 0)
    def _():
        for k in range(4):
            value = dot(hidden[: 3 * rows, :], down[k]).astype(BF)
            for r in range(3):
                outs[r][k][...] = value[r * rows : (r + 1) * rows]

    @pl.when(lax.axis_index("core") == 1)
    def _():
        for k in range(3):
            value = dot(hidden[...], down[k]).astype(BF)
            for r in range(4):
                outs[k][r][...] = value[r * rows : (r + 1) * rows]


def down_of(hidden, mine, theirs):
    rows, units = hidden.shape
    part = mine.shape[1] // 8
    return pl.pallas_call(
        down_kernel,
        in_specs=[VMEM, HBM, HBM],
        out_specs=[VMEM] * 5,
        out_shape=[jax.ShapeDtypeStruct((s, rows // 4, part), BF) for s in (2, 2, 2, 2, 4)],
        scratch_shapes=[pltpu.VMEM((4, units, part), BF), pltpu.SemaphoreType.DMA((8,))],
        compiler_params=pltpu.CompilerParams(vmem_limit_bytes=20 * MIB),
        cost_estimate=COST,
    )(hidden, mine, theirs)


def mid_kernel(own, high, low, got_1, got_3, mid_1, mid_3):
    for i, parts, out in ((1, (low.at[1], got_1), mid_1), (3, (high.at[1], got_3), mid_3)):
        total = own[i].astype(F32)
        for part in parts:
            total = total + part[...].astype(F32)
        out[...] = total.astype(BF)


def mid_sums(*values):
    piece = jax.ShapeDtypeStruct(values[-1].shape, BF)
    return pl.pallas_call(
        mid_kernel,
        in_specs=[VMEM] * 5,
        out_specs=[VMEM] * 2,
        out_shape=[piece, piece],
        compiler_params=pltpu.CompilerParams(vmem_limit_bytes=16 * MIB),
        cost_estimate=COST,
    )(*values)


def last_kernel(a, b, c, d, out):
    z = lax.axis_index("expert")
    for i, step in enumerate(sum(ROUTES, ())):
        total = a[i].astype(F32) + b[i].astype(F32) + c[i].astype(F32) + d[i].astype(F32)
        out[(z - step + 8) & 7] = total.astype(BF)


def last_sum(parts):
    shape = (E, CAP, parts[0].shape[1])
    return pl.pallas_call(
        last_kernel,
        in_specs=[VMEM] * 4,
        out_specs=VMEM,
        out_shape=jax.ShapeDtypeStruct(shape, BF),
        compiler_params=pltpu.CompilerParams(vmem_limit_bytes=16 * MIB),
        cost_estimate=COST,
    )(*[p.reshape(shape) for p in parts])


def body(tokens, routes, logits, w_gate, w_up, w_down):
    rows, width = tokens.shape
    half = width // 2
    part = half // 4
    y, c, z = lax.axis_index("ty"), lax.axis_index("core"), lax.axis_index("expert")

    ids = jnp.arange(E, dtype=jnp.int32)[:, None]
    chosen = routes.T[None, :, :] == ids[:, :, None]
    named = jnp.any(chosen, axis=1)
    numbers = jnp.arange(rows, dtype=jnp.int32)
    earlier = (numbers[:, None] < numbers[None, :]).astype(BF)
    before = dot(named.astype(BF), earlier)
    columns = lax.dynamic_slice_in_dim(tokens, c * half, half, 1)
    slots = jnp.arange(CAP, dtype=jnp.int32).astype(F32)
    line = jnp.where(c == 0, y, -y % 4)

    def outgoing(j):
        step = jnp.int32(ROUTES[0][j])
        for number in range(1, 4):
            step = jnp.where(line == number, ROUTES[number][j], step)
        expert = (z + step + 8) % 8
        row = lambda v: lax.dynamic_slice_in_dim(v, expert, 1, 0)
        hit = row(named) & (row(before) == slots[:, None])
        return dot(hit.astype(BF), columns).astype(BF)

    w_gate, w_up, w_down = w_gate[0], w_up[0], w_down[0]
    weights = [w_gate, w_up, swap(w_gate), swap(w_up)]
    downs = [w_down, swap(w_down)]
    arrived = [along_z(outgoing(j), j) for j in range(2)]
    piece = after(jnp.concatenate(arrived, axis=0), *weights[2:], downs[1])

    low = jnp.concatenate([piece, plane(piece, 0, 1)], axis=0)
    high = jnp.concatenate([plane(piece, 0, -1), plane(piece, 0, 2)], axis=0)
    below_low, above_low = plane(low, 1, 1), plane(low, 1, -1)
    below_high, above_high = plane(high, 1, 1), plane(high, 1, -1)
    own_sums = gate_up([low, high], (0, 2), weights)
    far = [plane(after(below_low, own_sums), 1, 1), plane(above_high, 1, -1)]
    near_sums = gate_up([below_low, above_low], (0, 2), weights)
    more_sums = gate_up([below_high, above_high], (0, 2), weights)
    sums = gate_up(
        far,
        (12, 14),
        weights,
        [own_sums, near_sums, more_sums],
        ((0, 0, 0), (0, 2, 2), (1, 0, 4), (1, 2, 8), (2, 0, 6), (2, 2, 10)),
    )
    hidden, far_a, far_b = hidden_of(sums, swap(sums), *downs)
    below_a, below_b, above_a, above_b, own = down_of(hidden, *downs)

    from_below, from_above = plane(far_a, 0, 1), plane(far_b, 0, -1)
    got_high, got_low = plane(above_b, 0, 1), plane(below_a, 0, -1)
    to_above = [add(above_a[i], from_below[i]) for i in range(2)]
    to_below = [add(below_b[i], from_above[i]) for i in range(2)]
    got_1, got_3 = plane(to_above[1], 0, 1), plane(to_below[1], 0, -1)
    got_0, got_2 = plane(to_above[0], 0, 1), plane(to_below[0], 0, -1)
    mid_1, mid_3 = mid_sums(own, got_high, got_low, got_1, got_3)
    end_3, end_1 = plane(mid_3, 1, 2), plane(mid_1, 1, -1)
    mid_0, mid_2 = add(own[0], got_low[0], got_0), add(own[2], got_high[0], got_2)
    ends = [mid_0, end_1, plane(mid_2, 1, 1), end_3]
    table = lax.all_to_all(last_sum(ends), "expert", 0, 0, tiled=True)
    table = table.reshape(E * CAP, part)

    share = jax.nn.sigmoid(logits - logits[:, ::-1])
    shares = jnp.sum(jnp.where(chosen, share.T[None, :, :], 0.0), axis=1)
    hit = named[:, None, :] & (before[:, None, :] == slots[None, :, None])
    mix = jnp.where(hit, shares[:, None, :], 0.0).reshape(E * CAP, rows)
    high_mix = mix.astype(BF)
    low_mix = (mix - high_mix.astype(F32)).astype(BF)
    back = lambda m: lax.dot_general(m, table, (((0,), (0,)), ((), ())), preferred_element_type=F32)
    return (back(high_mix) + back(low_mix)).astype(BF)


def solution(mesh):
    grid = Mesh(mesh.devices.reshape(4, 8, 4, 2), ("dp", "expert", "ty", "core"))
    tensor = ("ty", "core")
    placed = (
        P(("dp", "expert"), None),
        P(("dp", "expert"), None),
        P(("dp", "expert"), None),
        P("expert", None, ("dp",) + tensor),
        P("expert", None, ("dp",) + tensor),
        P("expert", ("dp",) + tensor, None),
    )
    return jax.shard_map(
        body, mesh=grid, in_specs=placed, out_specs=P(("dp", "expert"), tensor), check_vma=False
    )
```
